32 devices in a mesh: runs: 2 (over x), space: 16 (over z, y, core).
Axes of the slice: x: 2, y: 2, z: 4, core: 2. Of those that a mesh axis runs over, the one named last changes fastest.
Arguments:
- phase_noise: float32 [32, 8, 16, 8, 128], P(('runs', 'space')), parts along dimension 0, may hold values from -0.9 to 0.9
- labels: int32 [64, 8, 128], P(('runs', 'space')), parts along dimension 0, may hold values from 0 to 63
- solute: float32 [64, 8, 128], P(('runs', 'space')), parts along dimension 0, may hold values from 0.05 to 0.95
- mobility: float32 [64], replicated, may hold values from 0.5 to 2
- phase_cotangent_blocks: float32 [32, 8, 16, 8, 128], P(('runs', 'space')), parts along dimension 0, may hold values from -6 to 6
- adj_solute: float32 [64, 8, 128], P(('runs', 'space')), parts along dimension 0, may hold values from -6 to 6
Outputs:
- grad_phase: float32 [32, 8, 16, 8, 128], P(('runs', 'space')), parts along dimension 0
- solute_gradient: float32 [64, 8, 128], P(('runs', 'space')), parts along dimension 0
- mobility_gradient: float32 [128], P('runs'), parts along dimension 0
The draws below stay inside these ranges and needn't reach their ends.
There are 2 independent parts, one for each index of `runs`. The reference program is written for one: setup_inputs(seed, part) draws one part's arguments, and reference() takes and returns one part's arrays. A program takes and returns all parts, laid end to end along the dimension named above; an argument that names none is the same for every part. Nothing has to cross between parts.
All inputs are finite; a program needn't handle non-finite values.
Results may differ from the reference program's by a relative error of at most 0.000022.
Values sent between devices are 32-bit elements; how exact they have to be, the bound alone decides.
A program may use at most 64 MiB of HBM per device.

```python
import math
import jax
import jax.numpy as jnp
from jax import lax

P_SIZE = 64
GROUPS = 8
CZ = 16
NX = 8
NY = 128
PL = 8
BLOCKS = 16
NZ = 32
N_SPACE = 16


def place_ends(drawn, own_key, smallest, top_value):
    spot = [jax.random.randint(jax.random.fold_in(own_key, axis), (), 0, length) for axis, length in enumerate(drawn.shape)]
    main_axis = drawn.shape.index(max(drawn.shape))
    neighbour = spot[:main_axis] + [(spot[main_axis] + 1) % drawn.shape[main_axis]] + spot[main_axis + 1:]
    return drawn.at[tuple(spot)].set(smallest).at[tuple(neighbour)].set(top_value)


def steps_of(stream_key, shape, shards, smallest, largest):
    def one(axis_at, shards_of):
        steps = jax.random.uniform(jax.random.fold_in(jax.random.fold_in(stream_key, 6), axis_at), (shards_of,), jnp.float32, smallest / len(shards), largest / len(shards))
        return jnp.repeat(jnp.exp(steps), shape[axis_at] // shards_of).reshape((-1,) + (1,) * (len(shape) - axis_at - 1))

    level = one(*shards[0])
    for cut in shards[1:]:
        level = level * one(*cut)
    return level


def scatter_about(rng, extent, width, limit, pieces=(), kind=jnp.bfloat16):
    values = width * jax.random.normal(rng, extent, jnp.float32)
    if pieces:
        values = values * steps_of(rng, extent, pieces, -0.22, 0.18)
    return jnp.clip(values, -limit, limit).astype(kind)


def setup_inputs(seed: int = 0, part: int = 0) -> dict:
    seeds = jax.random.split(jax.random.key(seed), 7)
    part_splits = jax.random.split(jax.random.fold_in(seeds[6], part), 7)
    phase_noise = scatter_about(part_splits[0], (BLOCKS, PL, CZ, NX, NY), 0.15, 0.9, ((0, 16),), jnp.float32)
    labels = place_ends(jax.random.randint(part_splits[1], (NZ, NX, NY), 0, P_SIZE), jax.random.fold_in(part_splits[1], 1), 0, P_SIZE - 1).astype(jnp.int32)
    solute = jnp.clip(0.05 + 0.9 * jax.random.uniform(part_splits[2], (NZ, NX, NY), jnp.float32) ** steps_of(part_splits[2], (NZ, NX, NY), ((0, 16),), -0.2, 0.2), 0.05, 0.95)
    mobility = jnp.clip(jnp.exp(jax.random.uniform(seeds[3], (P_SIZE,), jnp.float32, math.log(0.5), math.log(2.0))), 0.5, 2.0)
    phase_cotangent_blocks = scatter_about(part_splits[4], (BLOCKS, PL, CZ, NX, NY), 1.0, 6.0, ((0, 16),), jnp.float32)
    adj_solute = scatter_about(part_splits[5], (NZ, NX, NY), 1.0, 6.0, ((0, 16),), jnp.float32)
    return dict(phase_noise=phase_noise, labels=labels, solute=solute, mobility=mobility, phase_cotangent_blocks=phase_cotangent_blocks, adj_solute=adj_solute)


time_step = 0.1
gradient_coef = 0.75
well_height = 1.0
coupling = 1.5
chem_height = 2.5
alpha_level = 0.2
beta_level = 0.8
solute_mobility = 0.3
epsilon = 1e-05

def pointwise(phases, solute):
    orders = phases.shape[0]
    beta_mask = (jnp.arange(orders) >= orders // 2).astype(jnp.float32).reshape(orders, 1, 1, 1)
    squares = phases * phases
    total = lax.optimization_barrier(jnp.sum(squares, axis=0))
    denom = total + epsilon
    share = lax.optimization_barrier(jnp.sum(squares * beta_mask, axis=0)) / denom
    chem_slope = chem_height * ((solute - beta_level) ** 2 - (solute - alpha_level) ** 2)
    reaction = well_height * (phases ** 3 - phases + 2.0 * coupling * phases * (total - squares))
    reaction = reaction + chem_slope * 2.0 * phases * (beta_mask - share) / denom
    potential = 2.0 * chem_height * (solute - alpha_level - share * (beta_level - alpha_level))
    return (reaction, potential)

def laplace(field):
    result = -6.0 * field
    for axis in (-3, -2, -1):
        result = result + jnp.roll(field, 1, axis) + jnp.roll(field, -1, axis)
    return result

def advance(phases, solute, mobility):
    reaction, potential = pointwise(phases, solute)
    drive = reaction - gradient_coef * laplace(phases)
    phases_next = phases - time_step * mobility[:, None, None, None] * drive
    solute_next = solute + time_step * solute_mobility * laplace(potential)
    return (phases_next, solute_next)

def merge_blocks(blocked):
    slabs = N_SPACE // GROUPS
    shaped = blocked.reshape(slabs, GROUPS, PL, CZ, NX, NY).transpose(1, 2, 0, 3, 4, 5)
    return shaped.reshape(GROUPS * PL, slabs * CZ, NX, NY)

def split_into_blocks(natural_layout):
    slabs = N_SPACE // GROUPS
    shaped = natural_layout.reshape(GROUPS, PL, slabs, CZ, NX, NY).transpose(2, 0, 1, 3, 4, 5)
    return shaped.reshape(N_SPACE, PL, CZ, NX, NY)

def reference(phase_noise, labels, solute, mobility, phase_cotangent_blocks, adj_solute):
    noise = merge_blocks(phase_noise)
    adjoint = merge_blocks(phase_cotangent_blocks)
    orders = noise.shape[0]
    variants = jnp.arange(orders, dtype=jnp.int32).reshape(orders, 1, 1, 1)
    start = noise + 0.5 * (labels[None] == variants).astype(jnp.float32)

    def run(phases, conc, mobs):
        phases, conc = advance(phases, conc, mobs)
        phases, conc = advance(phases, conc, mobs)
        return (phases, conc)
    outputs, pullback = jax.vjp(run, start, solute, mobility)
    gradient_value, solute_gradient, mobility_gradient = pullback((adjoint, adj_solute))
    return (split_into_blocks(gradient_value), solute_gradient, mobility_gradient)
```

```python
import functools

import jax
import jax.numpy as jnp
from jax import lax
from jax.experimental import pallas as pl
from jax.experimental.pallas import tpu as pltpu
from jax.sharding import PartitionSpec as P

P_SIZE = 64
GROUPS = 8

time_step = 0.1
gradient_coef = 0.75
coupling = 1.5
chem_height = 2.5
alpha_level = 0.2
beta_level = 0.8
solute_mobility = 0.3
epsilon = 1e-05

MESH = pl.DeviceIdType.MESH
CUBIC = 1.0 - 2.0 * coupling
GAP = beta_level - alpha_level
BETA_GROUP = GROUPS // 2

LABELS, SUM_A, COEF_A, SUM_B, COEF_B, SUM_C, COEF_C, MOBILITY = range(8)
PHASE_RIM, ADJ_RIM, BAR_RIM, ADJ_RING, POT_RING, BAR_RING = range(6)


def turn(x):
    last = x.ndim - 1
    lanes, rows = x.shape[-1], x.shape[-2]
    across = pltpu.roll(x, 1, last) + pltpu.roll(x, lanes - 1, last)
    return across + (pltpu.roll(x, 1, last - 1) + pltpu.roll(x, rows - 1, last - 1))


def curve(ref, layer):
    middle = ref[:, layer + 1]
    return (ref[:, layer] + ref[:, layer + 2] - 6.0 * middle) + turn(middle)


def curve_cells(ref):
    middle = ref[1:-1]
    return (ref[:-2] + ref[2:] - 6.0 * middle) + turn(middle)


def kernel(
    slabs, noise_ref, labels_ref, solute_ref, mobility_ref, adj_ref, adjc_ref,
    grad_ref, solgrad_ref, mobgrad_ref,
    phi, lam, bar, phi1, drive, pre, rate_buf, lab, conc, adjc, pot, adjc1,
    sum_a, got_a, put_a, coef_a, sum_b, got_b, put_b, coef_b, sum_c, got_c, put_c, coef_c,
    mob_mine, mob_slabs, mob_all,
    load_sem, out_sem, send_sem, recv_sem, rim_send, rim_recv, mob_send, mob_recv,
):
    orders, layers = noise_ref.shape[0], noise_ref.shape[1]
    sub = layers // GROUPS
    place = lax.axis_index("space")
    count = slabs * GROUPS
    group = lax.rem(place, GROUPS)
    slab = lax.div(place, GROUPS)
    base = slab * GROUPS
    after, before = lax.rem(place + 1, count), lax.rem(place + count - 1, count)
    above, below = lax.rem(place + GROUPS, count), lax.rem(place + count - GROUPS, count)

    def peer(j):
        return lax.rem(group + j, GROUPS)

    def other_slab(s):
        return lax.rem(slab + s, slabs) * GROUPS + group

    barrier = pltpu.get_barrier_semaphore()
    for j in range(1, GROUPS):
        pl.semaphore_signal(barrier, inc=1, device_id={"space": base + peer(j)}, device_id_type=MESH)
    for s in range(1, slabs):
        pl.semaphore_signal(barrier, inc=1, device_id={"space": other_slab(s)}, device_id_type=MESH)
    for device in (after, before):
        pl.semaphore_signal(barrier, inc=1, device_id={"space": device}, device_id_type=MESH)

    load_labels = pltpu.make_async_copy(labels_ref, lab.at[group], load_sem.at[0])
    load_noise = pltpu.make_async_copy(noise_ref, phi.at[:, pl.ds(1, layers)], load_sem.at[1])
    load_adjc = pltpu.make_async_copy(adjc_ref, adjc.at[pl.ds(1, sub)], load_sem.at[2])
    load_solute = pltpu.make_async_copy(solute_ref, conc, load_sem.at[3])
    load_adj = pltpu.make_async_copy(adj_ref, lam.at[:, pl.ds(1, layers)], load_sem.at[4])
    for load in (load_labels, load_noise, load_adjc, load_solute, load_adj):
        load.start()
    for i in range(orders):
        rate_buf[i] = jnp.full(rate_buf.shape[1:], time_step * mobility_ref[group * orders + i], jnp.float32)

    pl.semaphore_wait(barrier, GROUPS - 1 + slabs - 1 + 2)

    def to_peer(kind, src, dst, p):
        return pltpu.make_async_remote_copy(
            src_ref=src, dst_ref=dst, send_sem=send_sem.at[kind, p], recv_sem=recv_sem.at[kind, group],
            device_id={"space": base + p}, device_id_type=MESH,
        )

    def arrived(kind, dst, p):
        pltpu.make_async_remote_copy(
            src_ref=dst, dst_ref=dst, send_sem=send_sem.at[kind, p], recv_sem=recv_sem.at[kind, p],
            device_id={"space": base + p}, device_id_type=MESH,
        ).wait_recv()

    def sent(kind, src, p):
        pltpu.make_async_remote_copy(
            src_ref=src, dst_ref=src, send_sem=send_sem.at[kind, p], recv_sem=recv_sem.at[kind, p],
            device_id={"space": base + p}, device_id_type=MESH,
        ).wait_send()

    def over_peers(act):
        def run(j, carry):
            act(peer(j))
            return carry

        lax.fori_loop(1, GROUPS, run, 0)

    def rim_copy(kind, side, src, dst, device):
        return pltpu.make_async_remote_copy(
            src_ref=src, dst_ref=dst, send_sem=rim_send.at[kind, side], recv_sem=rim_recv.at[kind, side],
            device_id={"space": device}, device_id_type=MESH,
        )

    def rims_of(kind, src, ref, offset):
        last = layers + 1
        return (
            rim_copy(kind, 0, src.at[:, layers - 1 + offset], ref.at[:, 0], above),
            rim_copy(kind, 1, src.at[:, offset], ref.at[:, last], below),
        )

    def ring_of(kind, src, ref, offset):
        return (
            rim_copy(kind, 0, src.at[sub - 1 + offset], ref.at[0], after),
            rim_copy(kind, 1, src.at[offset], ref.at[sub + 1], before),
        )

    over_peers(lambda p: to_peer(LABELS, labels_ref, lab.at[group], p).start())
    adj_ring = ring_of(ADJ_RING, adjc_ref, adjc, 0)
    adj_rim = rims_of(ADJ_RIM, adj_ref, lam, 0)
    for copy in adj_ring:
        copy.start()

    def start_chunk(p):
        for k in range(sub):
            z = p * sub + k
            ids = group * orders + lax.broadcasted_iota(jnp.int32, rate_buf.shape, 0)
            field = phi[:, z + 1] + jnp.where(lab[p, k][None] == ids, 0.5, 0.0)
            phi[:, z + 1] = field
            sum_a[p, k] = jnp.sum(field * field, axis=0)

    load_labels.wait()
    load_noise.wait()
    start_chunk(group)
    got_a[group] = sum_a[group]

    def start_peer(p):
        arrived(LABELS, lab.at[p], p)
        start_chunk(p)
        to_peer(SUM_A, sum_a.at[p], got_a.at[group], p).start()

    over_peers(start_peer)
    phase_rim = rims_of(PHASE_RIM, phi, phi, 1)
    for copy in phase_rim + adj_rim:
        copy.start()

    def local_drive(z):
        field = phi[:, z + 1]
        drive[:, z] = CUBIC * field * field * field - gradient_coef * curve(phi, z)

    def over_inner(act):
        def run(z, carry):
            act(z)
            return carry

        lax.fori_loop(1, layers - 1, run, 0)

    over_inner(local_drive)
    load_adjc.wait()
    load_solute.wait()
    load_adj.wait()
    for copy in adj_ring:
        copy.wait_recv()

    def total_of(parts):
        low, high = parts[0], parts[BETA_GROUP]
        for g in range(1, BETA_GROUP):
            low = low + parts[g]
            high = high + parts[BETA_GROUP + g]
        return low + high, high

    def state_of(squares, beta_squares, c):
        inverse = 1.0 / (squares + epsilon)
        share = beta_squares * inverse
        slope = chem_height * ((c - beta_level) ** 2 - (c - alpha_level) ** 2)
        pull = 2.0 * slope * inverse
        plain = 2.0 * coupling * squares - 1.0 - pull * share
        return inverse, share, pull, plain

    def adjoint_of(state, moment, beta_moment, pot_bar):
        inverse, share, pull, _ = state
        scaled = pull * inverse
        pot_part = (2.0 * chem_height * GAP) * inverse * pot_bar
        all_bar = 2.0 * coupling * moment - scaled * (beta_moment - 2.0 * share * moment) + share * pot_part
        beta_bar = -scaled * moment - pot_part
        c_bar = (-4.0 * chem_height * GAP) * inverse * (beta_moment - share * moment) + 2.0 * chem_height * pot_bar
        return 2.0 * all_bar, 2.0 * (all_bar + beta_bar), c_bar

    over_peers(lambda p: arrived(SUM_A, got_a.at[p], p))
    state_a = state_of(*total_of(got_a), conc[...])
    put_a[0] = state_a[3]
    put_a[1] = state_a[3] + state_a[2]
    over_peers(lambda p: to_peer(COEF_A, put_a.at[lax.div(p, BETA_GROUP)], coef_a.at[group], p).start())
    coef_a[group] = put_a[lax.div(group, BETA_GROUP)]
    pot[1 : sub + 1] = 2.0 * chem_height * (conc[...] - alpha_level - state_a[1] * GAP)
    pot_ring = ring_of(POT_RING, pot, pot, 1)
    for copy in pot_ring:
        copy.start()

    for copy in phase_rim:
        copy.wait_recv()
    local_drive(0)
    local_drive(layers - 1)

    def step_chunk(p):
        for k in range(sub):
            z = p * sub + k
            field = phi[:, z + 1]
            full = drive[:, z] + field * coef_a[p, k][None]
            drive[:, z] = full
            rate = rate_buf[...]
            following = field - rate * full
            phi1[:, z] = following
            sum_b[p, 0, k] = jnp.sum(following * following, axis=0)
            sum_b[p, 1, k] = -jnp.sum(rate * lam[:, z + 1] * following, axis=0)

    step_chunk(group)
    got_b[group] = sum_b[group]

    def step_peer(p):
        arrived(COEF_A, coef_a.at[p], p)
        step_chunk(p)
        to_peer(SUM_B, sum_b.at[p], got_b.at[group], p).start()

    over_peers(step_peer)

    def local_bar(z, moved):
        adj, field, rate = lam[:, z + 1], phi1[:, z], rate_buf[...]
        curved = gradient_coef * curve(lam, z)
        squared = field * field
        pre[:, z] = adj + rate * (curved - (3.0 * CUBIC) * squared * adj)
        return moved + field * (CUBIC * squared * adj - curved)

    moved = lax.fori_loop(1, layers - 1, local_bar, jnp.zeros(rate_buf.shape, jnp.float32))

    pot_bar_b = (time_step * solute_mobility) * curve_cells(adjc)
    for copy in pot_ring:
        copy.wait_recv()
    conc1 = conc[...] + (time_step * solute_mobility) * curve_cells(pot)
    over_peers(lambda p: arrived(SUM_B, got_b.at[p], p))
    state_b = state_of(*total_of([got_b[g, 0] for g in range(GROUPS)]), conc1)
    plain_b, beta_b, c_bar_b = adjoint_of(
        state_b, *total_of([got_b[g, 1] for g in range(GROUPS)]), pot_bar_b
    )
    put_b[0, 0] = state_b[3]
    put_b[0, 1] = plain_b
    put_b[1, 0] = state_b[3] + state_b[2]
    put_b[1, 1] = beta_b
    over_peers(lambda p: to_peer(COEF_B, put_b.at[lax.div(p, BETA_GROUP)], coef_b.at[group], p).start())
    coef_b[group] = put_b[lax.div(group, BETA_GROUP)]
    adjc1[1 : sub + 1] = adjc[1 : sub + 1] + c_bar_b
    bar_ring = ring_of(BAR_RING, adjc1, adjc1, 1)
    for copy in bar_ring:
        copy.start()

    for copy in adj_rim:
        copy.wait_recv()
    moved = local_bar(0, moved)
    moved = local_bar(layers - 1, moved)

    def bar_chunk(p, moved):
        for k in range(sub):
            z = p * sub + k
            adj, field, rate = lam[:, z + 1], phi1[:, z], rate_buf[...]
            scaled = adj * coef_b[p, 0, k][None]
            full = pre[:, z] + field * coef_b[p, 1, k][None] - rate * scaled
            bar[:, z + 1] = full
            sum_c[p, k] = -jnp.sum(rate * full * phi[:, z + 1], axis=0)
            moved = moved + (field * scaled + full * drive[:, z])
        return moved

    moved = bar_chunk(group, moved)
    got_c[group] = sum_c[group]

    def bar_peer(j, moved):
        p = peer(j)
        arrived(COEF_B, coef_b.at[p], p)
        moved = bar_chunk(p, moved)
        to_peer(SUM_C, sum_c.at[p], got_c.at[group], p).start()
        return moved

    moved = lax.fori_loop(1, GROUPS, bar_peer, moved)
    bar_rim = rims_of(BAR_RIM, bar, bar, 1)
    for copy in bar_rim:
        copy.start()
    mob_mine[...] = -time_step * jnp.sum(moved, axis=1)
    mob_copies = [
        pltpu.make_async_remote_copy(
            src_ref=mob_mine, dst_ref=mob_slabs.at[s - 1], send_sem=mob_send.at[s - 1], recv_sem=mob_recv.at[s - 1],
            device_id={"space": other_slab(s)}, device_id_type=MESH,
        )
        for s in range(1, slabs)
    ]
    for copy in mob_copies:
        copy.start()

    def local_grad(z):
        full, field, rate = bar[:, z + 1], phi[:, z + 1], rate_buf[...]
        p, k = z // sub, z % sub
        slope = coef_a[p, k][None] + (3.0 * CUBIC) * field * field
        pre[:, z] = full + rate * (gradient_coef * curve(bar, z) - full * slope)

    over_inner(local_grad)
    for copy in bar_ring:
        copy.wait_recv()
    pot_bar_a = (time_step * solute_mobility) * curve_cells(adjc1)
    over_peers(lambda p: arrived(SUM_C, got_c.at[p], p))
    plain_c, beta_c, c_bar_a = adjoint_of(state_a, *total_of(got_c), pot_bar_a)
    put_c[0] = plain_c
    put_c[1] = beta_c
    over_peers(lambda p: to_peer(COEF_C, put_c.at[lax.div(p, BETA_GROUP)], coef_c.at[group], p).start())
    coef_c[group] = put_c[lax.div(group, BETA_GROUP)]
    solgrad_ref[...] = adjc1[1 : sub + 1] + c_bar_a

    for copy in mob_copies:
        copy.wait_recv()
    whole = mob_mine[...]
    for s in range(1, slabs):
        whole = whole + mob_slabs[s - 1]
    mob_all[group] = whole
    over_peers(lambda p: to_peer(MOBILITY, mob_all.at[group], mob_all.at[group], p).start())

    for copy in bar_rim:
        copy.wait_recv()
    local_grad(0)
    local_grad(layers - 1)

    def store(p):
        rows = pl.ds(p * sub, sub)
        return pltpu.make_async_copy(pre.at[:, rows], grad_ref.at[:, rows], out_sem.at[p])

    def grad_chunk(p):
        for k in range(sub):
            z = p * sub + k
            pre[:, z] = pre[:, z] + phi[:, z + 1] * coef_c[p, k][None]
        store(p).start()

    grad_chunk(group)

    def grad_peer(p):
        arrived(COEF_C, coef_c.at[p], p)
        grad_chunk(p)

    over_peers(grad_peer)
    over_peers(lambda p: arrived(MOBILITY, mob_all.at[p], p))
    table = mob_all[...].reshape(GROUPS * orders, mob_all.shape[-1])
    mobgrad_ref[...] = jnp.sum(table.T, axis=0, keepdims=True)

    def finish(p):
        sent(LABELS, labels_ref, p)
        sent(SUM_A, sum_a.at[p], p)
        sent(COEF_A, put_a.at[0], p)
        sent(SUM_B, sum_b.at[p], p)
        sent(COEF_B, put_b.at[0], p)
        sent(SUM_C, sum_c.at[p], p)
        sent(COEF_C, put_c.at[0], p)
        sent(MOBILITY, mob_all.at[group], p)
        store(p).wait()

    over_peers(finish)
    store(group).wait()
    for copy in adj_ring + adj_rim + phase_rim + pot_ring + bar_ring + bar_rim + tuple(mob_copies):
        copy.wait_send()


def body(slabs, phase_noise, labels, solute, mobility, cotangent, adj_solute):
    _, orders, layers, rows, lanes = phase_noise.shape
    sub = labels.shape[0]
    tile = (rows, lanes)

    def vmem(*lead):
        return pltpu.VMEM(lead + tile, jnp.float32)

    anywhere = pl.BlockSpec(memory_space=pl.ANY)
    in_vmem = pl.BlockSpec(memory_space=pltpu.VMEM)
    elements = orders * layers * rows * lanes
    grad, solute_gradient, mobility_gradient = pl.pallas_call(
        functools.partial(kernel, slabs),
        out_shape=(
            jax.ShapeDtypeStruct(phase_noise.shape[1:], jnp.float32),
            jax.ShapeDtypeStruct(solute.shape, jnp.float32),
            jax.ShapeDtypeStruct((1, mobility.shape[0]), jnp.float32),
        ),
        in_specs=[anywhere, anywhere, anywhere, pl.BlockSpec(memory_space=pltpu.SMEM), anywhere, anywhere],
        out_specs=(anywhere, in_vmem, in_vmem),
        scratch_shapes=[
            vmem(orders, layers + 2), vmem(orders, layers + 2), vmem(orders, layers + 2),
            vmem(orders, layers), vmem(orders, layers), vmem(orders, layers), vmem(orders),
            pltpu.VMEM((GROUPS, sub) + tile, jnp.int32),
            vmem(sub), vmem(sub + 2), vmem(sub + 2), vmem(sub + 2),
            vmem(GROUPS, sub), vmem(GROUPS, sub), vmem(2, sub), vmem(GROUPS, sub),
            vmem(GROUPS, 2, sub), vmem(GROUPS, 2, sub), vmem(2, 2, sub), vmem(GROUPS, 2, sub),
            vmem(GROUPS, sub), vmem(GROUPS, sub), vmem(2, sub), vmem(GROUPS, sub),
            pltpu.VMEM((orders, lanes), jnp.float32),
            pltpu.VMEM((max(slabs - 1, 1), orders, lanes), jnp.float32),
            pltpu.VMEM((GROUPS, orders, lanes), jnp.float32),
            pltpu.SemaphoreType.DMA((5,)),
            pltpu.SemaphoreType.DMA((GROUPS,)),
            pltpu.SemaphoreType.DMA((8, GROUPS)),
            pltpu.SemaphoreType.DMA((8, GROUPS)),
            pltpu.SemaphoreType.DMA((6, 2)),
            pltpu.SemaphoreType.DMA((6, 2)),
            pltpu.SemaphoreType.DMA((max(slabs - 1, 1),)),
            pltpu.SemaphoreType.DMA((max(slabs - 1, 1),)),
        ],
        compiler_params=pltpu.CompilerParams(
            collective_id=0, has_side_effects=True, vmem_limit_bytes=24 * 1024 * 1024
        ),
        cost_estimate=pl.CostEstimate(flops=100 * elements, bytes_accessed=12 * elements, transcendentals=0),
    )(phase_noise[0], labels, solute, mobility, cotangent[0], adj_solute)
    return grad[None], solute_gradient, mobility_gradient.reshape(-1)


def solution(mesh):
    slabs = mesh.shape["space"] // GROUPS
    fields = P(("runs", "space"), None, None, None, None)
    cells = P(("runs", "space"), None, None)
    return jax.shard_map(
        functools.partial(body, slabs),
        mesh=mesh,
        in_specs=(fields, cells, cells, P(), fields, cells),
        out_specs=(fields, cells, P("runs")),
        check_vma=False,
    )
```

```python
import functools

import jax
import jax.numpy as jnp
from jax import lax
from jax.experimental import pallas as pl
from jax.experimental.pallas import tpu as pltpu
from jax.sharding import PartitionSpec as P

P_SIZE = 64
GROUPS = 8

time_step = 0.1
gradient_coef = 0.75
coupling = 1.5
chem_height = 2.5
alpha_level = 0.2
beta_level = 0.8
solute_mobility = 0.3
epsilon = 1e-05

MESH = pl.DeviceIdType.MESH
CUBIC = 1.0 - 2.0 * coupling
GAP = beta_level - alpha_level
BETA_GROUP = GROUPS // 2
PAIRS = GROUPS // 2
VMEM_LIMIT = 16 * 1024 * 1024

LABELS, SUM_A, COEF_A, SUM_B, COEF_B, SUM_C, COEF_C, MOBILITY = range(8)
PHASE_RIM, ADJ_RIM, BAR_RIM, ADJ_RING, POT_RING, BAR_RING, GIVE, GIVE_BACK = range(8)


def turn(x):
    last = x.ndim - 1
    lanes, rows = x.shape[-1], x.shape[-2]
    across = pltpu.roll(x, 1, last) + pltpu.roll(x, lanes - 1, last)
    return across + (pltpu.roll(x, 1, last - 1) + pltpu.roll(x, rows - 1, last - 1))


def curve(ref, layer):
    middle = ref[:, layer + 1]
    return (ref[:, layer] + ref[:, layer + 2] - 6.0 * middle) + turn(middle)


def curve_cells(ref):
    middle = ref[1:-1]
    return (ref[:-2] + ref[2:] - 6.0 * middle) + turn(middle)


def kernel(
    slabs, noise_ref, labels_ref, solute_ref, mobility_hbm, adj_ref, adjc_ref,
    grad_ref, solgrad_ref, mobgrad_ref,
    mobility_ref, phi, lam, bar, phi1, drive, pre, rate_buf, lab, conc, adjc, pot, adjc1,
    sum_a, got_a, put_a, coef_a, sum_b, got_b, put_b, coef_b, sum_c, got_c, put_c, coef_c,
    mob_mine, mob_slabs, mob_all, solgrad,
    load_sem, send_sem, recv_sem, rim_send, rim_recv, mob_send, mob_recv,
):
    orders, layers = noise_ref.shape[0], noise_ref.shape[1]
    sub = layers // GROUPS
    span = layers // PAIRS
    place = lax.axis_index("space")
    count = slabs * GROUPS
    group = lax.rem(place, GROUPS)
    slab = lax.div(place, GROUPS)
    base = slab * GROUPS
    pair = lax.div(group, 2)
    second = lax.rem(group, 2)
    owner = second == 1
    above, below = lax.rem(place + GROUPS, count), lax.rem(place + count - GROUPS, count)

    def pair_at(j):
        high = lax.rem(lax.div(pair, 2) + lax.div(j, 2), 2)
        low = lax.rem(lax.rem(pair, 2) + lax.rem(j, 2), 2)
        return 2 * high + low

    def far_pairs():
        return [pair_at(jnp.int32(j)) for j in range(PAIRS - 1, 0, -1)]

    def others():
        return [2 * q + c for q in far_pairs() for c in range(2)] + [2 * pair + 1 - second]

    def other_slab(s):
        return lax.rem(slab + s, slabs) * GROUPS + group

    def shifted(by):
        return lax.rem(place + count + by, count)

    barrier = pltpu.get_barrier_semaphore()

    def greet(device):
        pl.semaphore_signal(barrier, inc=1, device_id={"space": device}, device_id_type=MESH)

    for s in range(1, slabs):
        greet(other_slab(s))

    @pl.when(owner)
    def _():
        for by in (2, -2, 1):
            greet(shifted(by))

    for g in others():
        greet(base + g)

    load_labels = pltpu.make_async_copy(labels_ref, lab.at[pl.ds(group * sub, sub)], load_sem.at[0])
    load_noise = pltpu.make_async_copy(noise_ref, phi.at[:, pl.ds(1, layers)], load_sem.at[1])
    load_adjc = pltpu.make_async_copy(adjc_ref, adjc.at[pl.ds(1 + second * sub, sub)], load_sem.at[2])
    load_solute = pltpu.make_async_copy(solute_ref, conc.at[pl.ds(second * sub, sub)], load_sem.at[3])
    load_adj = pltpu.make_async_copy(adj_ref, lam.at[:, pl.ds(1, layers)], load_sem.at[4])
    load_mobility = pltpu.make_async_copy(mobility_hbm, mobility_ref, load_sem.at[5])
    for load in (load_mobility, load_labels, load_noise, load_adjc, load_solute, load_adj):
        load.start()
    load_mobility.wait()
    for i in range(orders):
        rate_buf[i] = jnp.full(rate_buf.shape[1:], time_step * mobility_ref[group * orders + i], jnp.float32)

    pl.semaphore_wait(barrier, GROUPS - 1 + slabs - 1 + 1 + second)

    def to_group(kind, src, dst, g, slot):
        return pltpu.make_async_remote_copy(
            src_ref=src, dst_ref=dst, send_sem=send_sem.at[kind, g], recv_sem=recv_sem.at[kind, slot],
            device_id={"space": base + g}, device_id_type=MESH,
        )

    def arrived(kind, dst, slot):
        to_group(kind, dst, dst, 2 * pair + 1 - second, slot).wait_recv()

    def sent(kind, src, g):
        to_group(kind, src, src, g, g).wait_send()

    def rim_copy(kind, side, src, dst, device):
        return pltpu.make_async_remote_copy(
            src_ref=src, dst_ref=dst, send_sem=rim_send.at[kind, side], recv_sem=rim_recv.at[kind, side],
            device_id={"space": device}, device_id_type=MESH,
        )

    def rims_of(kind, src, ref, offset):
        last = layers + 1
        return (
            rim_copy(kind, 0, src.at[:, layers - 1 + offset], ref.at[:, 0], above),
            rim_copy(kind, 1, src.at[:, offset], ref.at[:, last], below),
        )

    def ring_of(kind, ref):
        return (
            rim_copy(kind, 0, ref.at[span], ref.at[0], shifted(2)),
            rim_copy(kind, 1, ref.at[1], ref.at[span + 1], shifted(-2)),
        )

    sibling = shifted(1 - 2 * second)
    adj_down = rim_copy(ADJ_RING, 1, adjc_ref.at[0], adjc.at[span + 1], shifted(-1))
    adj_up = rim_copy(ADJ_RING, 0, adjc_ref.at[sub - 1], adjc.at[0], shifted(2))
    give_adjc = rim_copy(GIVE, 0, adjc_ref, adjc.at[pl.ds(1, sub)], sibling)
    give_solute = rim_copy(GIVE, 1, solute_ref, conc.at[pl.ds(0, sub)], sibling)
    pot_ring = ring_of(POT_RING, pot)
    bar_ring = ring_of(BAR_RING, adjc1)
    give_solgrad = rim_copy(GIVE_BACK, 0, solgrad.at[pl.ds(0, sub)], solgrad.at[pl.ds(0, sub)], sibling)

    for g in others():
        to_group(LABELS, labels_ref, lab.at[pl.ds(group * sub, sub)], g, group).start()

    @pl.when(owner)
    def _():
        adj_up.start()

    @pl.when(second == 0)
    def _():
        give_solute.start()
        give_adjc.start()
        adj_down.start()

    adj_rim = rims_of(ADJ_RIM, adj_ref, lam, 0)

    def labels_from(g):
        arrived(LABELS, lab.at[pl.ds(g * sub, sub)], g)

    def over_layers(q, act):
        for k in range(span):
            act(q * span + k, k)

    def give_sum(kind, sums, got, q):
        to_group(kind, sums.at[q], got.at[group], 2 * q + 1, group).start()

    def over_pairs(kind, sums, got, chunk, carry):
        def run(i, carry):
            q = pair_at(PAIRS - 1 - i)
            carry = chunk(q, True, carry)
            give_sum(kind, sums, got, q)
            return carry

        carry = lax.fori_loop(0, PAIRS - 1, run, carry)
        carry = chunk(pair, False, carry)

        @pl.when(second == 0)
        def _():
            give_sum(kind, sums, got, pair)

        @pl.when(owner)
        def _():
            got[group] = sums[pair]

        return carry

    def all_sums(kind, got):
        for g in others():
            arrived(kind, got.at[g], g)

    def give_coef(kind, put, coef):
        for g in others():
            to_group(kind, put.at[lax.div(g, BETA_GROUP)], coef.at[pair], g, pair).start()
        coef[pair] = put[lax.div(group, BETA_GROUP)]

    def own_coef(kind, coef):
        @pl.when(second == 0)
        def _():
            arrived(kind, coef.at[pair], pair)

    def start_chunk(q, far, carry):
        if far:
            labels_from(2 * q)
            labels_from(2 * q + 1)
        else:
            labels_from(2 * pair + 1 - second)

        def layer(z, k):
            ids = group * orders + lax.broadcasted_iota(jnp.int32, rate_buf.shape, 0)
            field = phi[:, z + 1] + jnp.where(lab[z][None] == ids, 0.5, 0.0)
            phi[:, z + 1] = field
            sum_a[q, k] = jnp.sum(field * field, axis=0)

        over_layers(q, layer)
        return carry

    load_labels.wait()
    load_noise.wait()
    over_pairs(SUM_A, sum_a, got_a, start_chunk, 0)
    phase_rim = rims_of(PHASE_RIM, phi, phi, 1)
    for copy in phase_rim + adj_rim:
        copy.start()

    def local_drive(z):
        field = phi[:, z + 1]
        drive[:, z] = CUBIC * field * field * field - gradient_coef * curve(phi, z)

    def over_inner(act):
        def run(z, carry):
            act(z)
            return carry

        lax.fori_loop(1, layers - 1, run, 0)

    over_inner(local_drive)
    load_adjc.wait()
    load_solute.wait()
    load_adj.wait()

    def total_of(parts):
        low, high = parts[0], parts[BETA_GROUP]
        for g in range(1, BETA_GROUP):
            low = low + parts[g]
            high = high + parts[BETA_GROUP + g]
        return low + high, high

    def state_of(squares, beta_squares, c):
        inverse = 1.0 / (squares + epsilon)
        share = beta_squares * inverse
        slope = chem_height * ((c - beta_level) ** 2 - (c - alpha_level) ** 2)
        pull = 2.0 * slope * inverse
        plain = 2.0 * coupling * squares - 1.0 - pull * share
        return inverse, share, pull, plain

    def adjoint_of(state, moment, beta_moment, pot_bar):
        inverse, share, pull, _ = state
        scaled = pull * inverse
        pot_part = (2.0 * chem_height * GAP) * inverse * pot_bar
        all_bar = 2.0 * coupling * moment - scaled * (beta_moment - 2.0 * share * moment) + share * pot_part
        beta_bar = -scaled * moment - pot_part
        c_bar = (-4.0 * chem_height * GAP) * inverse * (beta_moment - share * moment) + 2.0 * chem_height * pot_bar
        return 2.0 * all_bar, 2.0 * (all_bar + beta_bar), c_bar

    @pl.when(owner)
    def _():
        give_solute.wait_recv()
        all_sums(SUM_A, got_a)
        state = state_of(*total_of(got_a), conc[...])
        put_a[0] = state[3]
        put_a[1] = state[3] + state[2]
        give_coef(COEF_A, put_a, coef_a)
        pot[1 : span + 1] = 2.0 * chem_height * (conc[...] - alpha_level - state[1] * GAP)
        for copy in pot_ring:
            copy.start()

    for copy in phase_rim:
        copy.wait_recv()
    local_drive(0)
    local_drive(layers - 1)

    def step_chunk(q, far, carry):
        if far:
            arrived(COEF_A, coef_a.at[q], q)
        else:
            own_coef(COEF_A, coef_a)

        def layer(z, k):
            field = phi[:, z + 1]
            full = drive[:, z] + field * coef_a[q, k][None]
            drive[:, z] = full
            rate = rate_buf[...]
            following = field - rate * full
            phi1[:, z] = following
            sum_b[q, 0, k] = jnp.sum(following * following, axis=0)
            sum_b[q, 1, k] = -jnp.sum(rate * lam[:, z + 1] * following, axis=0)

        over_layers(q, layer)
        return carry

    over_pairs(SUM_B, sum_b, got_b, step_chunk, 0)

    def local_bar(z, moved):
        adj, field, rate = lam[:, z + 1], phi1[:, z], rate_buf[...]
        curved = gradient_coef * curve(lam, z)
        squared = field * field
        pre[:, z] = adj + rate * (curved - (3.0 * CUBIC) * squared * adj)
        return moved + field * (CUBIC * squared * adj - curved)

    moved = lax.fori_loop(1, layers - 1, local_bar, jnp.zeros(rate_buf.shape, jnp.float32))

    @pl.when(owner)
    def _():
        for copy in (give_adjc, adj_up, adj_down) + pot_ring:
            copy.wait_recv()
        pot_bar = (time_step * solute_mobility) * curve_cells(adjc)
        conc1 = conc[...] + (time_step * solute_mobility) * curve_cells(pot)
        all_sums(SUM_B, got_b)
        state = state_of(*total_of([got_b[g, 0] for g in range(GROUPS)]), conc1)
        plain, beta, c_bar = adjoint_of(state, *total_of([got_b[g, 1] for g in range(GROUPS)]), pot_bar)
        put_b[0, 0] = state[3]
        put_b[0, 1] = plain
        put_b[1, 0] = state[3] + state[2]
        put_b[1, 1] = beta
        give_coef(COEF_B, put_b, coef_b)
        adjc1[1 : span + 1] = adjc[1 : span + 1] + c_bar
        for copy in bar_ring:
            copy.start()

    for copy in adj_rim:
        copy.wait_recv()
    moved = local_bar(0, moved)
    moved = local_bar(layers - 1, moved)

    def bar_chunk(q, far, moved):
        if far:
            arrived(COEF_B, coef_b.at[q], q)
        else:
            own_coef(COEF_B, coef_b)
        for k in range(span):
            z = q * span + k
            adj, field, rate = lam[:, z + 1], phi1[:, z], rate_buf[...]
            scaled = adj * coef_b[q, 0, k][None]
            full = pre[:, z] + field * coef_b[q, 1, k][None] - rate * scaled
            bar[:, z + 1] = full
            sum_c[q, k] = -jnp.sum(rate * full * phi[:, z + 1], axis=0)
            moved = moved + (field * scaled + full * drive[:, z])
        return moved

    moved = over_pairs(SUM_C, sum_c, got_c, bar_chunk, moved)
    bar_rim = rims_of(BAR_RIM, bar, bar, 1)
    for copy in bar_rim:
        copy.start()
    mob_mine[...] = -time_step * jnp.sum(moved, axis=1)
    mob_copies = [
        pltpu.make_async_remote_copy(
            src_ref=mob_mine, dst_ref=mob_slabs.at[s - 1], send_sem=mob_send.at[s - 1], recv_sem=mob_recv.at[s - 1],
            device_id={"space": other_slab(s)}, device_id_type=MESH,
        )
        for s in range(1, slabs)
    ]
    for copy in mob_copies:
        copy.start()

    def local_grad(z):
        full, field, rate = bar[:, z + 1], phi[:, z + 1], rate_buf[...]
        slope = coef_a[z // span, z % span][None] + (3.0 * CUBIC) * field * field
        pre[:, z] = full + rate * (gradient_coef * curve(bar, z) - full * slope)

    over_inner(local_grad)

    @pl.when(owner)
    def _():
        for copy in bar_ring:
            copy.wait_recv()
        pot_bar = (time_step * solute_mobility) * curve_cells(adjc1)
        state = state_of(*total_of(got_a), conc[...])
        all_sums(SUM_C, got_c)
        plain, beta, c_bar = adjoint_of(state, *total_of(got_c), pot_bar)
        put_c[0] = plain
        put_c[1] = beta
        give_coef(COEF_C, put_c, coef_c)
        solgrad[...] = adjc1[1 : span + 1] + c_bar
        give_solgrad.start()

    for copy in mob_copies:
        copy.wait_recv()
    whole = mob_mine[...]
    for s in range(1, slabs):
        whole = whole + mob_slabs[s - 1]
    mob_all[group] = whole
    for g in others():
        to_group(MOBILITY, mob_all.at[group], mob_all.at[group], g, group).start()

    for copy in bar_rim:
        copy.wait_recv()
    local_grad(0)
    local_grad(layers - 1)

    def grad_chunk(q):
        def layer(z, k):
            grad_ref[:, z] = pre[:, z] + phi[:, z + 1] * coef_c[q, k][None]

        over_layers(q, layer)

    own_coef(COEF_C, coef_c)
    grad_chunk(pair)

    def grad_pair(j, carry):
        q = pair_at(j)
        arrived(COEF_C, coef_c.at[q], q)
        grad_chunk(q)
        return carry

    lax.fori_loop(1, PAIRS, grad_pair, 0)

    @pl.when(second == 0)
    def _():
        give_solgrad.wait_recv()

    solgrad_ref[...] = solgrad[pl.ds(second * sub, sub)]
    for g in others():
        arrived(MOBILITY, mob_all.at[g], g)
    table = mob_all[...].reshape(GROUPS * orders, mob_all.shape[-1])
    mobgrad_ref[...] = jnp.sum(table.T, axis=0, keepdims=True)

    for g in others():
        sent(LABELS, labels_ref, g)
        sent(MOBILITY, mob_all.at[group], g)
    for q in far_pairs():
        sent(SUM_A, sum_a.at[q], 2 * q + 1)
        sent(SUM_B, sum_b.at[q], 2 * q + 1)
        sent(SUM_C, sum_c.at[q], 2 * q + 1)

    @pl.when(second == 0)
    def _():
        for copy in (give_solute, give_adjc, adj_down):
            copy.wait_send()
        sent(SUM_A, sum_a.at[pair], 2 * pair + 1)
        sent(SUM_B, sum_b.at[pair], 2 * pair + 1)
        sent(SUM_C, sum_c.at[pair], 2 * pair + 1)

    @pl.when(owner)
    def _():
        for copy in (adj_up, give_solgrad) + pot_ring + bar_ring:
            copy.wait_send()
        for g in others():
            sent(COEF_A, put_a.at[0], g)
            sent(COEF_B, put_b.at[0], g)
            sent(COEF_C, put_c.at[0], g)

    for copy in adj_rim + phase_rim + bar_rim + tuple(mob_copies):
        copy.wait_send()


def hand_over(grad_in, solute_in, mobility_in, grad_out, solute_out, mobility_out, sem):
    copies = [pltpu.make_async_copy(solute_in, solute_out, sem.at[0])]
    copies.append(pltpu.make_async_copy(mobility_in, mobility_out, sem.at[1]))
    for i in range(grad_in.shape[0]):
        copies.append(pltpu.make_async_copy(grad_in.at[i], grad_out.at[i], sem.at[2 + i]))
    for copy in copies:
        copy.start()
    for copy in copies:
        copy.wait()


def body(slabs, phase_noise, labels, solute, mobility, cotangent, adj_solute):
    _, orders, layers, rows, lanes = phase_noise.shape
    sub = labels.shape[0]
    span = layers // PAIRS
    tile = (rows, lanes)

    def vmem(*lead):
        return pltpu.VMEM(lead + tile, jnp.float32)

    in_hbm = pl.BlockSpec(memory_space=pltpu.HBM)
    in_vmem = pl.BlockSpec(memory_space=pltpu.VMEM)
    elements = orders * layers * rows * lanes
    grad, solute_gradient, mobility_gradient = pl.pallas_call(
        functools.partial(kernel, slabs),
        out_shape=(
            jax.ShapeDtypeStruct(phase_noise.shape[1:], jnp.float32),
            jax.ShapeDtypeStruct(solute.shape, jnp.float32),
            jax.ShapeDtypeStruct((1, mobility.shape[0]), jnp.float32),
        ),
        in_specs=[in_hbm] * 6,
        out_specs=(in_vmem,) * 3,
        scratch_shapes=[
            pltpu.SMEM(mobility.shape, jnp.float32),
            vmem(orders, layers + 2), vmem(orders, layers + 2), vmem(orders, layers + 2),
            vmem(orders, layers), vmem(orders, layers), vmem(orders, layers), vmem(orders),
            pltpu.VMEM((layers,) + tile, jnp.int32),
            vmem(span), vmem(span + 2), vmem(span + 2), vmem(span + 2),
            vmem(PAIRS, span), vmem(GROUPS, span), vmem(2, span), vmem(PAIRS, span),
            vmem(PAIRS, 2, span), vmem(GROUPS, 2, span), vmem(2, 2, span), vmem(PAIRS, 2, span),
            vmem(PAIRS, span), vmem(GROUPS, span), vmem(2, span), vmem(PAIRS, span),
            pltpu.VMEM((orders, lanes), jnp.float32),
            pltpu.VMEM((max(slabs - 1, 1), orders, lanes), jnp.float32),
            pltpu.VMEM((GROUPS, orders, lanes), jnp.float32),
            vmem(span),
            pltpu.SemaphoreType.DMA((6,)),
            pltpu.SemaphoreType.DMA((8, GROUPS)),
            pltpu.SemaphoreType.DMA((8, GROUPS)),
            pltpu.SemaphoreType.DMA((8, 2)),
            pltpu.SemaphoreType.DMA((8, 2)),
            pltpu.SemaphoreType.DMA((max(slabs - 1, 1),)),
            pltpu.SemaphoreType.DMA((max(slabs - 1, 1),)),
        ],
        compiler_params=pltpu.CompilerParams(
            collective_id=0, has_side_effects=True, vmem_limit_bytes=VMEM_LIMIT
        ),
        cost_estimate=pl.CostEstimate(flops=100 * elements, bytes_accessed=12 * elements, transcendentals=0),
    )(*(pltpu.with_memory_space_constraint(x, pltpu.HBM) for x in (phase_noise[0], labels, solute, mobility, cotangent[0], adj_solute)))
    grad, solute_gradient, mobility_gradient = pl.pallas_call(
        hand_over,
        out_shape=tuple(jax.ShapeDtypeStruct(x.shape, x.dtype) for x in (grad, solute_gradient, mobility_gradient)),
        in_specs=[in_vmem] * 3,
        out_specs=(in_hbm,) * 3,
        scratch_shapes=[pltpu.SemaphoreType.DMA((orders + 2,))],
        compiler_params=pltpu.CompilerParams(vmem_limit_bytes=VMEM_LIMIT),
        cost_estimate=pl.CostEstimate(flops=0, bytes_accessed=8 * elements, transcendentals=0),
    )(grad, solute_gradient, mobility_gradient)
    return grad[None], solute_gradient, mobility_gradient.reshape(-1)


def solution(mesh):
    slabs = mesh.shape["space"] // GROUPS
    fields = P(("runs", "space"), None, None, None, None)
    cells = P(("runs", "space"), None, None)
    return jax.shard_map(
        functools.partial(body, slabs),
        mesh=mesh,
        in_specs=(fields, cells, cells, P(), fields, cells),
        out_specs=(fields, cells, P("runs")),
        check_vma=False,
    )
```

```python
import functools

import jax
import jax.numpy as jnp
from jax import lax
from jax.experimental import pallas as pl
from jax.experimental.pallas import tpu as pltpu
from jax.sharding import PartitionSpec as P

P_SIZE = 64
GROUPS = 8

time_step = 0.1
gradient_coef = 0.75
coupling = 1.5
chem_height = 2.5
alpha_level = 0.2
beta_level = 0.8
solute_mobility = 0.3
epsilon = 1e-05

MESH = pl.DeviceIdType.MESH
CUBIC = 1.0 - 2.0 * coupling
GAP = beta_level - alpha_level
BETA_GROUP = GROUPS // 2
PAIRS = GROUPS // 2
VMEM_LIMIT = 16 * 1024 * 1024

LABELS, SUM_A, COEF_A, SUM_B, COEF_B, SUM_C, COEF_C, MOBILITY, SUM_END = range(9)
PHASE_RIM, ADJ_RIM, BAR_RIM, ADJ_RING, POT_RING, BAR_RING, GIVE, GIVE_BACK, LABEL_RIM = range(9)


def turn(x):
    last = x.ndim - 1
    lanes, rows = x.shape[-1], x.shape[-2]
    across = pltpu.roll(x, 1, last) + pltpu.roll(x, lanes - 1, last)
    return across + (pltpu.roll(x, 1, last - 1) + pltpu.roll(x, rows - 1, last - 1))


def curve(ref, layer):
    middle = ref[:, layer + 1]
    return (ref[:, layer] + ref[:, layer + 2] - 6.0 * middle) + turn(middle)


def curve_cells(ref):
    middle = ref[1:-1]
    return (ref[:-2] + ref[2:] - 6.0 * middle) + turn(middle)


def kernel(
    slabs, noise_ref, labels_ref, solute_ref, mobility_hbm, adj_ref, adjc_ref,
    grad_ref, solgrad_ref, mobgrad_ref,
    mobility_ref, phi, lam, bar, phi1, drive, pre, rate_buf, lab, lab_rim, conc, adjc, pot, adjc1,
    sum_a, got_a, put_a, coef_a, sum_b, got_b, put_b, coef_b, sum_c, got_c, put_c, coef_c,
    mob_mine, mob_slabs, mob_all, solgrad,
    load_sem, send_sem, recv_sem, rim_send, rim_recv, mob_send, mob_recv,
):
    orders, layers = noise_ref.shape[0], noise_ref.shape[1]
    sub = layers // GROUPS
    span = layers // PAIRS
    place = lax.axis_index("space")
    count = slabs * GROUPS
    group = lax.rem(place, GROUPS)
    slab = lax.div(place, GROUPS)
    base = slab * GROUPS
    pair = lax.div(group, 2)
    second = lax.rem(group, 2)
    owner = second == 1
    above, below = lax.rem(place + GROUPS, count), lax.rem(place + count - GROUPS, count)

    def pair_at(j):
        high = lax.rem(lax.div(pair, 2) + lax.div(j, 2), 2)
        low = lax.rem(lax.rem(pair, 2) + lax.rem(j, 2), 2)
        return 2 * high + low

    def far_pairs():
        return [pair_at(jnp.int32(j)) for j in range(PAIRS - 1, 0, -1)]

    def others():
        return [2 * q + c for q in far_pairs() for c in range(2)] + [2 * pair + 1 - second]

    def other_slab(s):
        return lax.rem(slab + s, slabs) * GROUPS + group

    def shifted(by):
        return lax.rem(place + count + by, count)

    barrier = pltpu.get_barrier_semaphore()

    def greet(device):
        pl.semaphore_signal(barrier, inc=1, device_id={"space": device}, device_id_type=MESH)

    for s in range(1, slabs):
        greet(other_slab(s))

    @pl.when(owner)
    def _():
        for by in (2, -2, 1):
            greet(shifted(by))

    for g in others():
        greet(base + g)

    load_labels = pltpu.make_async_copy(labels_ref, lab.at[pl.ds(group * sub, sub)], load_sem.at[0])
    load_noise = pltpu.make_async_copy(noise_ref, phi.at[:, pl.ds(1, layers)], load_sem.at[1])
    load_adjc = pltpu.make_async_copy(adjc_ref, adjc.at[pl.ds(1 + second * sub, sub)], load_sem.at[2])
    load_solute = pltpu.make_async_copy(solute_ref, conc.at[pl.ds(second * sub, sub)], load_sem.at[3])
    load_adj = pltpu.make_async_copy(adj_ref, lam.at[:, pl.ds(1, layers)], load_sem.at[4])
    load_mobility = pltpu.make_async_copy(mobility_hbm, mobility_ref, load_sem.at[5])
    for load in (load_mobility, load_labels, load_noise, load_adjc, load_solute, load_adj):
        load.start()
    load_mobility.wait()
    for i in range(orders):
        rate_buf[i] = jnp.full(rate_buf.shape[1:], time_step * mobility_ref[group * orders + i], jnp.float32)

    pl.semaphore_wait(barrier, GROUPS - 1 + slabs - 1 + 1 + second)

    def to_group(kind, src, dst, g, slot):
        return pltpu.make_async_remote_copy(
            src_ref=src, dst_ref=dst, send_sem=send_sem.at[kind, g], recv_sem=recv_sem.at[kind, slot],
            device_id={"space": base + g}, device_id_type=MESH,
        )

    def arrived(kind, dst, slot):
        to_group(kind, dst, dst, 2 * pair + 1 - second, slot).wait_recv()

    def sent(kind, src, g):
        to_group(kind, src, src, g, g).wait_send()

    def rim_copy(kind, side, src, dst, device):
        return pltpu.make_async_remote_copy(
            src_ref=src, dst_ref=dst, send_sem=rim_send.at[kind, side], recv_sem=rim_recv.at[kind, side],
            device_id={"space": device}, device_id_type=MESH,
        )

    def rims_of(kind, src, ref, offset):
        last = layers + 1
        return (
            rim_copy(kind, 0, src.at[:, layers - 1 + offset], ref.at[:, 0], above),
            rim_copy(kind, 1, src.at[:, offset], ref.at[:, last], below),
        )

    def ring_of(kind, ref):
        return (
            rim_copy(kind, 0, ref.at[span], ref.at[0], shifted(2)),
            rim_copy(kind, 1, ref.at[1], ref.at[span + 1], shifted(-2)),
        )

    sibling = shifted(1 - 2 * second)
    adj_down = rim_copy(ADJ_RING, 1, adjc_ref.at[0], adjc.at[span + 1], shifted(-1))
    adj_up = rim_copy(ADJ_RING, 0, adjc_ref.at[sub - 1], adjc.at[0], shifted(2))
    give_adjc = rim_copy(GIVE, 0, adjc_ref, adjc.at[pl.ds(1, sub)], sibling)
    give_solute = rim_copy(GIVE, 1, solute_ref, conc.at[pl.ds(0, sub)], sibling)
    pot_ring = ring_of(POT_RING, pot)
    bar_ring = ring_of(BAR_RING, adjc1)
    give_solgrad = rim_copy(GIVE_BACK, 0, solgrad.at[pl.ds(0, sub)], solgrad.at[pl.ds(0, sub)], sibling)

    for g in others():
        to_group(LABELS, labels_ref, lab.at[pl.ds(group * sub, sub)], g, group).start()

    @pl.when(owner)
    def _():
        adj_up.start()

    @pl.when(second == 0)
    def _():
        give_solute.start()
        give_adjc.start()
        adj_down.start()

    phase_rim = rims_of(PHASE_RIM, noise_ref, phi, 0)
    adj_rim = rims_of(ADJ_RIM, adj_ref, lam, 0)
    label_rim = (
        rim_copy(LABEL_RIM, 0, lab.at[layers - 1], lab_rim.at[0], above),
        rim_copy(LABEL_RIM, 1, lab.at[0], lab_rim.at[1], below),
    )
    for copy in phase_rim:
        copy.start()

    def labels_from(g):
        arrived(LABELS, lab.at[pl.ds(g * sub, sub)], g)

    def over_layers(q, act):
        for k in range(span):
            act(q * span + k, k)

    def give_sum(kind, sums, got, q):
        to_group(kind, sums.at[q], got.at[group], 2 * q + 1, group).start()

    def over_pairs(kind, sums, got, chunk, carry):
        def run(i, carry):
            q = pair_at(PAIRS - 1 - i)
            carry = chunk(q, True, carry)
            give_sum(kind, sums, got, q)
            return carry

        carry = lax.fori_loop(0, PAIRS - 1, run, carry)
        carry = chunk(pair, False, carry)

        @pl.when(second == 0)
        def _():
            give_sum(kind, sums, got, pair)

        @pl.when(owner)
        def _():
            got[group] = sums[pair]

        return carry

    def all_sums(kind, got):
        for g in others():
            arrived(kind, got.at[g], g)

    def give_coef(kind, put, coef):
        for g in others():
            to_group(kind, put.at[lax.div(g, BETA_GROUP)], coef.at[pair], g, pair).start()
        coef[pair] = put[lax.div(group, BETA_GROUP)]

    def own_coef(kind, coef):
        @pl.when(second == 0)
        def _():
            arrived(kind, coef.at[pair], pair)

    def started(at, label):
        ids = group * orders + lax.broadcasted_iota(jnp.int32, rate_buf.shape, 0)
        field = phi[:, at] + jnp.where(label[None] == ids, 0.5, 0.0)
        phi[:, at] = field
        return field

    def start_chunk(q, far, carry):
        if far:
            labels_from(2 * q)
            labels_from(2 * q + 1)
        else:
            labels_from(2 * pair + 1 - second)

        def layer(z, k):
            field = started(z + 1, lab[z])
            sum_a[q, k] = jnp.sum(field * field, axis=0)

        over_layers(q, layer)
        return carry

    load_labels.wait()
    load_noise.wait()
    over_pairs(SUM_A, sum_a, got_a, start_chunk, 0)
    for copy in label_rim:
        copy.start()

    def local_layer(z):
        field, rate = phi[:, z + 1], rate_buf[...]
        push = CUBIC * field * field * field - gradient_coef * curve(phi, z)
        drive[:, z] = push
        known = field - rate * push
        phi1[:, z] = known
        scaled, adj = rate * field, rate * lam[:, z + 1]
        q, k = z // span, z % span
        sum_b[q, k, 0] = jnp.sum(known * known, axis=0)
        sum_b[q, k, 1] = jnp.sum(scaled * known, axis=0)
        sum_b[q, k, 2] = jnp.sum(scaled * scaled, axis=0)
        sum_b[q, k, 3] = jnp.sum(adj * known, axis=0)
        sum_b[q, k, 4] = jnp.sum(adj * scaled, axis=0)

    def inner_part(q):
        first = 1 if q == 0 else 0
        return pl.ds(first, span - 1 if q in (0, PAIRS - 1) else span)

    def end_part(q):
        return pl.ds(0 if q == 0 else span - 1, 1)

    def give_part(kind, q, part):
        @pl.when(2 * q + 1 != group)
        def _():
            to_group(kind, sum_b.at[q, part], got_b.at[group, part], 2 * q + 1, group).start()

        @pl.when(2 * q + 1 == group)
        def _():
            got_b[group, part] = sum_b[q, part]

    def sent_part(kind, q, part):
        @pl.when(2 * q + 1 != group)
        def _():
            sent(kind, sum_b.at[q, part], 2 * q + 1)

    def over_inner(act):
        def run(z, carry):
            act(z)
            return carry

        lax.fori_loop(1, layers - 1, run, 0)

    load_adj.wait()

    for q in (0, PAIRS - 1) + tuple(range(1, PAIRS - 1)):
        first = max(q * span, 1)
        last = min((q + 1) * span, layers - 1)

        def run(z, carry):
            local_layer(z)
            return carry

        lax.fori_loop(first, last, run, 0)
        give_part(SUM_B, q, inner_part(q))

    load_adjc.wait()
    load_solute.wait()

    def total_of(parts):
        low, high = parts[0], parts[BETA_GROUP]
        for g in range(1, BETA_GROUP):
            low = low + parts[g]
            high = high + parts[BETA_GROUP + g]
        return low + high, high

    def state_of(squares, beta_squares, c):
        inverse = 1.0 / (squares + epsilon)
        share = beta_squares * inverse
        slope = chem_height * ((c - beta_level) ** 2 - (c - alpha_level) ** 2)
        pull = 2.0 * slope * inverse
        plain = 2.0 * coupling * squares - 1.0 - pull * share
        return inverse, share, pull, plain

    def adjoint_of(state, moment, beta_moment, pot_bar):
        inverse, share, pull, _ = state
        scaled = pull * inverse
        pot_part = (2.0 * chem_height * GAP) * inverse * pot_bar
        all_bar = 2.0 * coupling * moment - scaled * (beta_moment - 2.0 * share * moment) + share * pot_part
        beta_bar = -scaled * moment - pot_part
        c_bar = (-4.0 * chem_height * GAP) * inverse * (beta_moment - share * moment) + 2.0 * chem_height * pot_bar
        return 2.0 * all_bar, 2.0 * (all_bar + beta_bar), c_bar

    @pl.when(owner)
    def _():
        give_solute.wait_recv()
        all_sums(SUM_A, got_a)
        state = state_of(*total_of(got_a), conc[...])
        put_a[0] = state[3]
        put_a[1] = state[3] + state[2]
        give_coef(COEF_A, put_a, coef_a)
        pot[1 : span + 1] = 2.0 * chem_height * (conc[...] - alpha_level - state[1] * GAP)
        for copy in pot_ring:
            copy.start()

    for copy in phase_rim + label_rim:
        copy.wait_recv()
    started(0, lab_rim[0])
    started(layers + 1, lab_rim[1])

    for q in (0, PAIRS - 1):
        local_layer(q * (layers - 1) // (PAIRS - 1))
        give_part(SUM_END, q, end_part(q))

    for copy in adj_rim:
        copy.start()

    @pl.when(owner)
    def _():
        for copy in (give_adjc, adj_up, adj_down) + pot_ring:
            copy.wait_recv()
        pot_bar = (time_step * solute_mobility) * curve_cells(adjc)
        conc1 = conc[...] + (time_step * solute_mobility) * curve_cells(pot)
        for q in range(PAIRS):

            @pl.when(pair == q)
            def _():
                for g in others():
                    arrived(SUM_B, got_b.at[g, inner_part(q)], g)
                if q in (0, PAIRS - 1):
                    for g in others():
                        arrived(SUM_END, got_b.at[g, end_part(q)], g)

        def plane(first, a):
            parts = [got_b[first] + got_b[first + 1], got_b[first + 2] + got_b[first + 3]]
            sums = parts[0] + parts[1]
            return sums[:, 0] - a * (2.0 * sums[:, 1] - a * sums[:, 2]), a * sums[:, 4] - sums[:, 3]

        low_squares, low_moment = plane(0, put_a[0])
        squares, moment = plane(BETA_GROUP, put_a[1])
        state = state_of(low_squares + squares, squares, conc1)
        plain, beta, c_bar = adjoint_of(state, low_moment + moment, moment, pot_bar)
        put_b[0, 0] = state[3]
        put_b[0, 1] = plain
        put_b[1, 0] = state[3] + state[2]
        put_b[1, 1] = beta
        give_coef(COEF_B, put_b, coef_b)
        adjc1[1 : span + 1] = adjc[1 : span + 1] + c_bar
        for copy in bar_ring:
            copy.start()

    def step_chunk(q):
        def layer(z, k):
            part = phi[:, z + 1] * coef_a[q, k][None]
            drive[:, z] = drive[:, z] + part
            phi1[:, z] = phi1[:, z] - rate_buf[...] * part

        over_layers(q, layer)

    own_coef(COEF_A, coef_a)
    step_chunk(pair)

    def step_pair(j, carry):
        q = pair_at(j)
        arrived(COEF_A, coef_a.at[q], q)
        step_chunk(q)
        return carry

    lax.fori_loop(1, PAIRS, step_pair, 0)

    def local_bar(z, moved):
        adj, field, rate = lam[:, z + 1], phi1[:, z], rate_buf[...]
        curved = gradient_coef * curve(lam, z)
        squared = field * field
        pre[:, z] = adj + rate * (curved - (3.0 * CUBIC) * squared * adj)
        return moved + field * (CUBIC * squared * adj - curved)

    moved = lax.fori_loop(1, layers - 1, local_bar, jnp.zeros(rate_buf.shape, jnp.float32))

    for copy in adj_rim:
        copy.wait_recv()
    moved = local_bar(0, moved)
    moved = local_bar(layers - 1, moved)

    def bar_chunk(q, moved):
        for k in range(span):
            z = q * span + k
            adj, field, rate = lam[:, z + 1], phi1[:, z], rate_buf[...]
            scaled = adj * coef_b[q, 0, k][None]
            full = pre[:, z] + field * coef_b[q, 1, k][None] - rate * scaled
            bar[:, z + 1] = full
            sum_c[q, k] = -jnp.sum(rate * full * phi[:, z + 1], axis=0)
            moved = moved + (field * scaled + full * drive[:, z])
        return moved

    bar_rim = rims_of(BAR_RIM, bar, bar, 1)

    def end_pair_sums(q):
        @pl.when(2 * q + 1 != group)
        def _():
            give_sum(SUM_C, sum_c, got_c, q)

        @pl.when(2 * q + 1 == group)
        def _():
            got_c[group] = sum_c[q]

    for step, q in enumerate((PAIRS - 1, 0) + tuple(range(1, PAIRS - 1))):

        @pl.when(2 * q + 1 != group)
        def _():
            arrived(COEF_B, coef_b.at[q], q)

        moved = bar_chunk(q, moved)
        end_pair_sums(q)
        if step < 2:
            bar_rim[step].start()
    mob_mine[...] = -time_step * jnp.sum(moved, axis=1)
    mob_copies = [
        pltpu.make_async_remote_copy(
            src_ref=mob_mine, dst_ref=mob_slabs.at[s - 1], send_sem=mob_send.at[s - 1], recv_sem=mob_recv.at[s - 1],
            device_id={"space": other_slab(s)}, device_id_type=MESH,
        )
        for s in range(1, slabs)
    ]
    for copy in mob_copies:
        copy.start()

    def local_grad(z):
        full, field, rate = bar[:, z + 1], phi[:, z + 1], rate_buf[...]
        slope = coef_a[z // span, z % span][None] + (3.0 * CUBIC) * field * field
        pre[:, z] = full + rate * (gradient_coef * curve(bar, z) - full * slope)

    over_inner(local_grad)

    @pl.when(owner)
    def _():
        for copy in bar_ring:
            copy.wait_recv()
        pot_bar = (time_step * solute_mobility) * curve_cells(adjc1)
        state = state_of(*total_of(got_a), conc[...])
        all_sums(SUM_C, got_c)
        plain, beta, c_bar = adjoint_of(state, *total_of(got_c), pot_bar)
        put_c[0] = plain
        put_c[1] = beta
        give_coef(COEF_C, put_c, coef_c)
        solgrad[...] = adjc1[1 : span + 1] + c_bar
        give_solgrad.start()

    for copy in mob_copies:
        copy.wait_recv()
    whole = mob_mine[...]
    for s in range(1, slabs):
        whole = whole + mob_slabs[s - 1]
    mob_all[group] = whole
    for g in others():
        to_group(MOBILITY, mob_all.at[group], mob_all.at[group], g, group).start()

    for copy in bar_rim:
        copy.wait_recv()
    local_grad(0)
    local_grad(layers - 1)

    def grad_chunk(q):
        def layer(z, k):
            grad_ref[:, z] = pre[:, z] + phi[:, z + 1] * coef_c[q, k][None]

        over_layers(q, layer)

    own_coef(COEF_C, coef_c)
    grad_chunk(pair)

    def grad_pair(j, carry):
        q = pair_at(j)
        arrived(COEF_C, coef_c.at[q], q)
        grad_chunk(q)
        return carry

    lax.fori_loop(1, PAIRS, grad_pair, 0)

    @pl.when(second == 0)
    def _():
        give_solgrad.wait_recv()

    solgrad_ref[...] = solgrad[pl.ds(second * sub, sub)]
    for g in others():
        arrived(MOBILITY, mob_all.at[g], g)
    table = mob_all[...].reshape(GROUPS * orders, mob_all.shape[-1])
    mobgrad_ref[...] = jnp.sum(table.T, axis=0, keepdims=True)

    for q in range(PAIRS):
        sent_part(SUM_B, q, inner_part(q))
        if q in (0, PAIRS - 1):
            sent_part(SUM_END, q, end_part(q))
    for g in others():
        sent(LABELS, labels_ref, g)
        sent(MOBILITY, mob_all.at[group], g)
    for q in far_pairs():
        sent(SUM_A, sum_a.at[q], 2 * q + 1)
        sent(SUM_C, sum_c.at[q], 2 * q + 1)

    @pl.when(second == 0)
    def _():
        for copy in (give_solute, give_adjc, adj_down):
            copy.wait_send()
        sent(SUM_A, sum_a.at[pair], 2 * pair + 1)
        sent(SUM_C, sum_c.at[pair], 2 * pair + 1)

    @pl.when(owner)
    def _():
        for copy in (adj_up, give_solgrad) + pot_ring + bar_ring:
            copy.wait_send()
        for g in others():
            sent(COEF_A, put_a.at[0], g)
            sent(COEF_B, put_b.at[0], g)
            sent(COEF_C, put_c.at[0], g)

    for copy in adj_rim + phase_rim + label_rim + bar_rim + tuple(mob_copies):
        copy.wait_send()


def hand_over(grad_in, solute_in, mobility_in, grad_out, solute_out, mobility_out, sem):
    copies = [pltpu.make_async_copy(solute_in, solute_out, sem.at[0])]
    copies.append(pltpu.make_async_copy(mobility_in, mobility_out, sem.at[1]))
    for i in range(grad_in.shape[0]):
        copies.append(pltpu.make_async_copy(grad_in.at[i], grad_out.at[i], sem.at[2 + i]))
    for copy in copies:
        copy.start()
    for copy in copies:
        copy.wait()


def body(slabs, phase_noise, labels, solute, mobility, cotangent, adj_solute):
    _, orders, layers, rows, lanes = phase_noise.shape
    sub = labels.shape[0]
    span = layers // PAIRS
    tile = (rows, lanes)

    def vmem(*lead):
        return pltpu.VMEM(lead + tile, jnp.float32)

    in_hbm = pl.BlockSpec(memory_space=pltpu.HBM)
    in_vmem = pl.BlockSpec(memory_space=pltpu.VMEM)
    elements = orders * layers * rows * lanes
    grad, solute_gradient, mobility_gradient = pl.pallas_call(
        functools.partial(kernel, slabs),
        out_shape=(
            jax.ShapeDtypeStruct(phase_noise.shape[1:], jnp.float32),
            jax.ShapeDtypeStruct(solute.shape, jnp.float32),
            jax.ShapeDtypeStruct((1, mobility.shape[0]), jnp.float32),
        ),
        in_specs=[in_hbm] * 6,
        out_specs=(in_vmem,) * 3,
        scratch_shapes=[
            pltpu.SMEM(mobility.shape, jnp.float32),
            vmem(orders, layers + 2), vmem(orders, layers + 2), vmem(orders, layers + 2),
            vmem(orders, layers), vmem(orders, layers), vmem(orders, layers), vmem(orders),
            pltpu.VMEM((layers,) + tile, jnp.int32), pltpu.VMEM((2,) + tile, jnp.int32),
            vmem(span), vmem(span + 2), vmem(span + 2), vmem(span + 2),
            vmem(PAIRS, span), vmem(GROUPS, span), vmem(2, span), vmem(PAIRS, span),
            vmem(PAIRS, span, 5), vmem(GROUPS, span, 5), vmem(2, 2, span), vmem(PAIRS, 2, span),
            vmem(PAIRS, span), vmem(GROUPS, span), vmem(2, span), vmem(PAIRS, span),
            pltpu.VMEM((orders, lanes), jnp.float32),
            pltpu.VMEM((max(slabs - 1, 1), orders, lanes), jnp.float32),
            pltpu.VMEM((GROUPS, orders, lanes), jnp.float32),
            vmem(span),
            pltpu.SemaphoreType.DMA((6,)),
            pltpu.SemaphoreType.DMA((9, GROUPS)),
            pltpu.SemaphoreType.DMA((9, GROUPS)),
            pltpu.SemaphoreType.DMA((9, 2)),
            pltpu.SemaphoreType.DMA((9, 2)),
            pltpu.SemaphoreType.DMA((max(slabs - 1, 1),)),
            pltpu.SemaphoreType.DMA((max(slabs - 1, 1),)),
        ],
        compiler_params=pltpu.CompilerParams(
            collective_id=0, has_side_effects=True, vmem_limit_bytes=VMEM_LIMIT
        ),
        cost_estimate=pl.CostEstimate(flops=100 * elements, bytes_accessed=12 * elements, transcendentals=0),
    )(*(pltpu.with_memory_space_constraint(x, pltpu.HBM) for x in (phase_noise[0], labels, solute, mobility, cotangent[0], adj_solute)))
    grad, solute_gradient, mobility_gradient = pl.pallas_call(
        hand_over,
        out_shape=tuple(jax.ShapeDtypeStruct(x.shape, x.dtype) for x in (grad, solute_gradient, mobility_gradient)),
        in_specs=[in_vmem] * 3,
        out_specs=(in_hbm,) * 3,
        scratch_shapes=[pltpu.SemaphoreType.DMA((orders + 2,))],
        compiler_params=pltpu.CompilerParams(vmem_limit_bytes=VMEM_LIMIT),
        cost_estimate=pl.CostEstimate(flops=0, bytes_accessed=8 * elements, transcendentals=0),
    )(grad, solute_gradient, mobility_gradient)
    return grad[None], solute_gradient, mobility_gradient.reshape(-1)


def solution(mesh):
    slabs = mesh.shape["space"] // GROUPS
    fields = P(("runs", "space"), None, None, None, None)
    cells = P(("runs", "space"), None, None)
    return jax.shard_map(
        functools.partial(body, slabs),
        mesh=mesh,
        in_specs=(fields, cells, cells, P(), fields, cells),
        out_specs=(fields, cells, P("runs")),
        check_vma=False,
    )
```

```python
import functools

import jax
import jax.numpy as jnp
from jax import lax
from jax.experimental import pallas as pl
from jax.experimental.pallas import tpu as pltpu
from jax.sharding import PartitionSpec as P

P_SIZE = 64
GROUPS = 8

time_step = 0.1
gradient_coef = 0.75
coupling = 1.5
chem_height = 2.5
alpha_level = 0.2
beta_level = 0.8
solute_mobility = 0.3
epsilon = 1e-05

MESH = pl.DeviceIdType.MESH
CUBIC = 1.0 - 2.0 * coupling
GAP = beta_level - alpha_level
BETA_GROUP = GROUPS // 2
PAIRS = GROUPS // 2
VMEM_LIMIT = 16 * 1024 * 1024

LABELS, SUM_A, COEF_A, SUM_B, COEF_B, SUM_C, COEF_C, MOBILITY, SUM_END = range(9)
PHASE_RIM, ADJ_RIM, BAR_RIM, ADJ_RING, POT_RING, BAR_RING, GIVE, GIVE_BACK, LABEL_RIM = range(9)


def turn(x):
    last = x.ndim - 1
    lanes, rows = x.shape[-1], x.shape[-2]
    across = pltpu.roll(x, 1, last) + pltpu.roll(x, lanes - 1, last)
    return across + (pltpu.roll(x, 1, last - 1) + pltpu.roll(x, rows - 1, last - 1))


def curve(ref, layer):
    middle = ref[:, layer + 1]
    return (ref[:, layer] + ref[:, layer + 2] - 6.0 * middle) + turn(middle)


def curve_cells(ref):
    middle = ref[1:-1]
    return (ref[:-2] + ref[2:] - 6.0 * middle) + turn(middle)


def kernel(
    slabs, noise_ref, labels_ref, solute_ref, mobility_hbm, adj_ref, adjc_ref,
    grad_ref, solgrad_ref, mobgrad_ref,
    mobility_ref, phi, lam, bar, phi1, drive, pre, rate_buf, lab, lab_rim, conc, adjc, pot, adjc1,
    sum_a, got_a, put_a, coef_a, sum_b, got_b, put_b, coef_b, sum_c, got_c, put_c, coef_c,
    mob_mine, mob_slabs, mob_all, solgrad,
    load_sem, send_sem, recv_sem, rim_send, rim_recv, mob_send, mob_recv,
):
    orders, layers = noise_ref.shape[0], noise_ref.shape[1]
    sub = layers // GROUPS
    span = layers // PAIRS
    place = lax.axis_index("space")
    count = slabs * GROUPS
    group = lax.rem(place, GROUPS)
    slab = lax.div(place, GROUPS)
    base = slab * GROUPS
    pair = lax.div(group, 2)
    second = lax.rem(group, 2)
    owner = second == 1
    above, below = lax.rem(place + GROUPS, count), lax.rem(place + count - GROUPS, count)

    def pair_at(j):
        high = lax.rem(lax.div(pair, 2) + lax.div(j, 2), 2)
        low = lax.rem(lax.rem(pair, 2) + lax.rem(j, 2), 2)
        return 2 * high + low

    def far_pairs():
        return [pair_at(jnp.int32(j)) for j in range(PAIRS - 1, 0, -1)]

    def others():
        return [2 * q + c for q in far_pairs() for c in range(2)] + [2 * pair + 1 - second]

    def other_slab(s):
        return lax.rem(slab + s, slabs) * GROUPS + group

    def shifted(by):
        return lax.rem(place + count + by, count)

    barrier = pltpu.get_barrier_semaphore()

    def greet(device):
        pl.semaphore_signal(barrier, inc=1, device_id={"space": device}, device_id_type=MESH)

    for s in range(1, slabs):
        greet(other_slab(s))

    @pl.when(owner)
    def _():
        for by in (2, -2, 1):
            greet(shifted(by))

    for g in others():
        greet(base + g)

    load_labels = pltpu.make_async_copy(labels_ref, lab.at[pl.ds(group * sub, sub)], load_sem.at[0])
    load_noise = pltpu.make_async_copy(noise_ref, phi.at[:, pl.ds(1, layers)], load_sem.at[1])
    load_adjc = pltpu.make_async_copy(adjc_ref, adjc.at[pl.ds(1 + second * sub, sub)], load_sem.at[2])
    load_solute = pltpu.make_async_copy(solute_ref, conc.at[pl.ds(second * sub, sub)], load_sem.at[3])
    load_adj = pltpu.make_async_copy(adj_ref, lam.at[:, pl.ds(1, layers)], load_sem.at[4])
    load_mobility = pltpu.make_async_copy(mobility_hbm, mobility_ref, load_sem.at[5])
    for load in (load_mobility, load_labels, load_noise, load_adjc, load_solute, load_adj):
        load.start()
    load_mobility.wait()
    for i in range(orders):
        rate_buf[i] = jnp.full(rate_buf.shape[1:], time_step * mobility_ref[group * orders + i], jnp.float32)

    pl.semaphore_wait(barrier, GROUPS - 1 + slabs - 1 + 1 + second)

    def to_group(kind, src, dst, g, slot):
        return pltpu.make_async_remote_copy(
            src_ref=src, dst_ref=dst, send_sem=send_sem.at[kind, g], recv_sem=recv_sem.at[kind, slot],
            device_id={"space": base + g}, device_id_type=MESH,
        )

    def arrived(kind, dst, slot):
        to_group(kind, dst, dst, 2 * pair + 1 - second, slot).wait_recv()

    def sent(kind, src, g):
        to_group(kind, src, src, g, g).wait_send()

    def rim_copy(kind, side, src, dst, device):
        return pltpu.make_async_remote_copy(
            src_ref=src, dst_ref=dst, send_sem=rim_send.at[kind, side], recv_sem=rim_recv.at[kind, side],
            device_id={"space": device}, device_id_type=MESH,
        )

    def rims_of(kind, src, ref, offset):
        last = layers + 1
        return (
            rim_copy(kind, 0, src.at[:, layers - 1 + offset], ref.at[:, 0], above),
            rim_copy(kind, 1, src.at[:, offset], ref.at[:, last], below),
        )

    def ring_of(kind, ref):
        return (
            rim_copy(kind, 0, ref.at[span], ref.at[0], shifted(2)),
            rim_copy(kind, 1, ref.at[1], ref.at[span + 1], shifted(-2)),
        )

    sibling = shifted(1 - 2 * second)
    adj_down = rim_copy(ADJ_RING, 1, adjc_ref.at[0], adjc.at[span + 1], shifted(-1))
    adj_up = rim_copy(ADJ_RING, 0, adjc_ref.at[sub - 1], adjc.at[0], shifted(2))
    give_adjc = rim_copy(GIVE, 0, adjc_ref, adjc.at[pl.ds(1, sub)], sibling)
    give_solute = rim_copy(GIVE, 1, solute_ref, conc.at[pl.ds(0, sub)], sibling)
    pot_ring = ring_of(POT_RING, pot)
    bar_ring = ring_of(BAR_RING, adjc1)
    give_solgrad = rim_copy(GIVE_BACK, 0, solgrad.at[pl.ds(0, sub)], solgrad.at[pl.ds(0, sub)], sibling)

    for g in others():
        to_group(LABELS, labels_ref, lab.at[pl.ds(group * sub, sub)], g, group).start()

    @pl.when(owner)
    def _():
        adj_up.start()

    @pl.when(second == 0)
    def _():
        give_solute.start()
        give_adjc.start()
        adj_down.start()

    phase_rim = rims_of(PHASE_RIM, noise_ref, phi, 0)
    adj_rim = rims_of(ADJ_RIM, adj_ref, lam, 0)
    label_rim = (
        rim_copy(LABEL_RIM, 0, lab.at[layers - 1], lab_rim.at[0], above),
        rim_copy(LABEL_RIM, 1, lab.at[0], lab_rim.at[1], below),
    )
    for copy in phase_rim:
        copy.start()

    def labels_from(g):
        arrived(LABELS, lab.at[pl.ds(g * sub, sub)], g)

    def over_layers(q, act):
        for k in range(span):
            act(q * span + k, k)

    def give_sum(kind, sums, got, q):
        to_group(kind, sums.at[q], got.at[group], 2 * q + 1, group).start()

    def over_pairs(kind, sums, got, chunk, carry):
        def run(i, carry):
            q = pair_at(PAIRS - 1 - i)
            carry = chunk(q, True, carry)
            give_sum(kind, sums, got, q)
            return carry

        carry = lax.fori_loop(0, PAIRS - 1, run, carry)
        carry = chunk(pair, False, carry)

        @pl.when(second == 0)
        def _():
            give_sum(kind, sums, got, pair)

        @pl.when(owner)
        def _():
            got[group] = sums[pair]

        return carry

    def all_sums(kind, got):
        for g in others():
            arrived(kind, got.at[g], g)

    def give_coef(kind, put, coef):
        for g in others():
            to_group(kind, put.at[lax.div(g, BETA_GROUP)], coef.at[pair], g, pair).start()
        coef[pair] = put[lax.div(group, BETA_GROUP)]

    def own_coef(kind, coef):
        @pl.when(second == 0)
        def _():
            arrived(kind, coef.at[pair], pair)

    def started(at, label):
        ids = group * orders + lax.broadcasted_iota(jnp.int32, rate_buf.shape, 0)
        field = phi[:, at] + jnp.where(label[None] == ids, 0.5, 0.0)
        phi[:, at] = field
        return field

    def start_chunk(q, far, carry):
        if far:
            labels_from(2 * q)
            labels_from(2 * q + 1)
        else:
            labels_from(2 * pair + 1 - second)

        def layer(z, k):
            field = started(z + 1, lab[z])
            sum_a[q, k] = jnp.sum(field * field, axis=0)

        over_layers(q, layer)
        return carry

    load_labels.wait()
    load_noise.wait()
    over_pairs(SUM_A, sum_a, got_a, start_chunk, 0)
    for copy in label_rim:
        copy.start()

    def local_layer(z):
        field, rate = phi[:, z + 1], rate_buf[...]
        push = CUBIC * field * field * field - gradient_coef * curve(phi, z)
        drive[:, z] = push
        known = field - rate * push
        phi1[:, z] = known
        scaled, adj = rate * field, rate * lam[:, z + 1]
        q, k = z // span, z % span
        sum_b[q, k, 0] = jnp.sum(known * known, axis=0)
        sum_b[q, k, 1] = jnp.sum(scaled * known, axis=0)
        sum_b[q, k, 2] = jnp.sum(scaled * scaled, axis=0)
        sum_b[q, k, 3] = jnp.sum(adj * known, axis=0)
        sum_b[q, k, 4] = jnp.sum(adj * scaled, axis=0)

    def inner_part(q):
        first = 1 if q == 0 else 0
        return pl.ds(first, span - 1 if q in (0, PAIRS - 1) else span)

    def end_part(q):
        return pl.ds(0 if q == 0 else span - 1, 1)

    def give_part(kind, q, part):
        @pl.when(2 * q + 1 != group)
        def _():
            to_group(kind, sum_b.at[q, part], got_b.at[group, part], 2 * q + 1, group).start()

        @pl.when(2 * q + 1 == group)
        def _():
            got_b[group, part] = sum_b[q, part]

    def sent_part(kind, q, part):
        @pl.when(2 * q + 1 != group)
        def _():
            sent(kind, sum_b.at[q, part], 2 * q + 1)

    def over_inner(act):
        def run(z, carry):
            act(z)
            return carry

        lax.fori_loop(1, layers - 1, run, 0)

    load_adj.wait()

    for q in (0, PAIRS - 1) + tuple(range(1, PAIRS - 1)):
        first = max(q * span, 1)
        last = min((q + 1) * span, layers - 1)

        def run(z, carry):
            local_layer(z)
            return carry

        lax.fori_loop(first, last, run, 0)
        give_part(SUM_B, q, inner_part(q))

    load_adjc.wait()
    load_solute.wait()

    def total_of(parts):
        low, high = parts[0], parts[BETA_GROUP]
        for g in range(1, BETA_GROUP):
            low = low + parts[g]
            high = high + parts[BETA_GROUP + g]
        return low + high, high

    def state_of(squares, beta_squares, c):
        inverse = 1.0 / (squares + epsilon)
        share = beta_squares * inverse
        slope = chem_height * ((c - beta_level) ** 2 - (c - alpha_level) ** 2)
        pull = 2.0 * slope * inverse
        plain = 2.0 * coupling * squares - 1.0 - pull * share
        return inverse, share, pull, plain

    def adjoint_of(state, moment, beta_moment, pot_bar):
        inverse, share, pull, _ = state
        scaled = pull * inverse
        pot_part = (2.0 * chem_height * GAP) * inverse * pot_bar
        all_bar = 2.0 * coupling * moment - scaled * (beta_moment - 2.0 * share * moment) + share * pot_part
        beta_bar = -scaled * moment - pot_part
        c_bar = (-4.0 * chem_height * GAP) * inverse * (beta_moment - share * moment) + 2.0 * chem_height * pot_bar
        return 2.0 * all_bar, 2.0 * (all_bar + beta_bar), c_bar

    @pl.when(owner)
    def _():
        give_solute.wait_recv()
        all_sums(SUM_A, got_a)
        state = state_of(*total_of(got_a), conc[...])
        put_a[0] = state[3]
        put_a[1] = state[3] + state[2]
        pot[1 : span + 1] = 2.0 * chem_height * (conc[...] - alpha_level - state[1] * GAP)
        for copy in pot_ring:
            copy.start()

    for copy in phase_rim + label_rim:
        copy.wait_recv()
    started(0, lab_rim[0])
    started(layers + 1, lab_rim[1])

    for q in (0, PAIRS - 1):
        local_layer(q * (layers - 1) // (PAIRS - 1))
        give_part(SUM_END, q, end_part(q))

    for copy in adj_rim:
        copy.start()

    @pl.when(owner)
    def _():
        give_coef(COEF_A, put_a, coef_a)

    @pl.when(owner)
    def _():
        for copy in (give_adjc, adj_up, adj_down) + pot_ring:
            copy.wait_recv()
        pot_bar = (time_step * solute_mobility) * curve_cells(adjc)
        conc1 = conc[...] + (time_step * solute_mobility) * curve_cells(pot)
        for q in range(PAIRS):

            @pl.when(pair == q)
            def _():
                for g in others():
                    arrived(SUM_B, got_b.at[g, inner_part(q)], g)
                if q in (0, PAIRS - 1):
                    for g in others():
                        arrived(SUM_END, got_b.at[g, end_part(q)], g)

        def plane(first, a):
            parts = [got_b[first] + got_b[first + 1], got_b[first + 2] + got_b[first + 3]]
            sums = parts[0] + parts[1]
            return sums[:, 0] - a * (2.0 * sums[:, 1] - a * sums[:, 2]), a * sums[:, 4] - sums[:, 3]

        low_squares, low_moment = plane(0, put_a[0])
        squares, moment = plane(BETA_GROUP, put_a[1])
        state = state_of(low_squares + squares, squares, conc1)
        plain, beta, c_bar = adjoint_of(state, low_moment + moment, moment, pot_bar)
        put_b[0, 0] = state[3]
        put_b[0, 1] = plain
        put_b[1, 0] = state[3] + state[2]
        put_b[1, 1] = beta
        give_coef(COEF_B, put_b, coef_b)
        adjc1[1 : span + 1] = adjc[1 : span + 1] + c_bar
        for copy in bar_ring:
            copy.start()

    def step_chunk(q):
        def layer(z, k):
            part = phi[:, z + 1] * coef_a[q, k][None]
            drive[:, z] = drive[:, z] + part
            phi1[:, z] = phi1[:, z] - rate_buf[...] * part

        over_layers(q, layer)

    own_coef(COEF_A, coef_a)
    step_chunk(pair)

    def step_pair(j, carry):
        q = pair_at(j)
        arrived(COEF_A, coef_a.at[q], q)
        step_chunk(q)
        return carry

    lax.fori_loop(1, PAIRS, step_pair, 0)

    def local_bar(z, moved):
        adj, field, rate = lam[:, z + 1], phi1[:, z], rate_buf[...]
        curved = gradient_coef * curve(lam, z)
        squared = field * field
        pre[:, z] = adj + rate * (curved - (3.0 * CUBIC) * squared * adj)
        return moved + field * (CUBIC * squared * adj - curved)

    moved = lax.fori_loop(1, layers - 1, local_bar, jnp.zeros(rate_buf.shape, jnp.float32))

    for copy in adj_rim:
        copy.wait_recv()
    moved = local_bar(0, moved)
    moved = local_bar(layers - 1, moved)

    def bar_chunk(q, moved):
        for k in range(span):
            z = q * span + k
            adj, field, rate = lam[:, z + 1], phi1[:, z], rate_buf[...]
            scaled = adj * coef_b[q, 0, k][None]
            full = pre[:, z] + field * coef_b[q, 1, k][None] - rate * scaled
            bar[:, z + 1] = full
            sum_c[q, k] = -jnp.sum(rate * full * phi[:, z + 1], axis=0)
            moved = moved + (field * scaled + full * drive[:, z])
        return moved

    bar_rim = rims_of(BAR_RIM, bar, bar, 1)

    def end_pair_sums(q):
        @pl.when(2 * q + 1 != group)
        def _():
            give_sum(SUM_C, sum_c, got_c, q)

        @pl.when(2 * q + 1 == group)
        def _():
            got_c[group] = sum_c[q]

    for step, q in enumerate((PAIRS - 1, 0) + tuple(range(1, PAIRS - 1))):

        @pl.when(2 * q + 1 != group)
        def _():
            arrived(COEF_B, coef_b.at[q], q)

        moved = bar_chunk(q, moved)
        end_pair_sums(q)
        if step < 2:
            bar_rim[step].start()
    mob_mine[...] = -time_step * jnp.sum(moved, axis=1)
    mob_copies = [
        pltpu.make_async_remote_copy(
            src_ref=mob_mine, dst_ref=mob_slabs.at[s - 1], send_sem=mob_send.at[s - 1], recv_sem=mob_recv.at[s - 1],
            device_id={"space": other_slab(s)}, device_id_type=MESH,
        )
        for s in range(1, slabs)
    ]
    for copy in mob_copies:
        copy.start()

    def local_grad(z):
        full, field, rate = bar[:, z + 1], phi[:, z + 1], rate_buf[...]
        slope = coef_a[z // span, z % span][None] + (3.0 * CUBIC) * field * field
        pre[:, z] = full + rate * (gradient_coef * curve(bar, z) - full * slope)

    over_inner(local_grad)

    @pl.when(owner)
    def _():
        for copy in bar_ring:
            copy.wait_recv()
        pot_bar = (time_step * solute_mobility) * curve_cells(adjc1)
        state = state_of(*total_of(got_a), conc[...])
        all_sums(SUM_C, got_c)
        plain, beta, c_bar = adjoint_of(state, *total_of(got_c), pot_bar)
        put_c[0] = plain
        put_c[1] = beta
        give_coef(COEF_C, put_c, coef_c)
        solgrad[...] = adjc1[1 : span + 1] + c_bar
        give_solgrad.start()

    for copy in mob_copies:
        copy.wait_recv()
    whole = mob_mine[...]
    for s in range(1, slabs):
        whole = whole + mob_slabs[s - 1]
    mob_all[group] = whole
    for g in others():
        to_group(MOBILITY, mob_all.at[group], mob_all.at[group], g, group).start()

    for copy in bar_rim:
        copy.wait_recv()
    local_grad(0)
    local_grad(layers - 1)

    def grad_chunk(q):
        def layer(z, k):
            grad_ref[:, z] = pre[:, z] + phi[:, z + 1] * coef_c[q, k][None]

        over_layers(q, layer)

    own_coef(COEF_C, coef_c)
    grad_chunk(pair)

    def grad_pair(j, carry):
        q = pair_at(j)
        arrived(COEF_C, coef_c.at[q], q)
        grad_chunk(q)
        return carry

    lax.fori_loop(1, PAIRS, grad_pair, 0)

    @pl.when(second == 0)
    def _():
        give_solgrad.wait_recv()

    solgrad_ref[...] = solgrad[pl.ds(second * sub, sub)]
    for g in others():
        arrived(MOBILITY, mob_all.at[g], g)
    table = mob_all[...].reshape(GROUPS * orders, mob_all.shape[-1])
    mobgrad_ref[...] = jnp.sum(table.T, axis=0, keepdims=True)

    for q in range(PAIRS):
        sent_part(SUM_B, q, inner_part(q))
        if q in (0, PAIRS - 1):
            sent_part(SUM_END, q, end_part(q))
    for g in others():
        sent(LABELS, labels_ref, g)
        sent(MOBILITY, mob_all.at[group], g)
    for q in far_pairs():
        sent(SUM_A, sum_a.at[q], 2 * q + 1)
        sent(SUM_C, sum_c.at[q], 2 * q + 1)

    @pl.when(second == 0)
    def _():
        for copy in (give_solute, give_adjc, adj_down):
            copy.wait_send()
        sent(SUM_A, sum_a.at[pair], 2 * pair + 1)
        sent(SUM_C, sum_c.at[pair], 2 * pair + 1)

    @pl.when(owner)
    def _():
        for copy in (adj_up, give_solgrad) + pot_ring + bar_ring:
            copy.wait_send()
        for g in others():
            sent(COEF_A, put_a.at[0], g)
            sent(COEF_B, put_b.at[0], g)
            sent(COEF_C, put_c.at[0], g)

    for copy in adj_rim + phase_rim + label_rim + bar_rim + tuple(mob_copies):
        copy.wait_send()


def hand_over(grad_in, solute_in, mobility_in, grad_out, solute_out, mobility_out, sem):
    copies = [pltpu.make_async_copy(solute_in, solute_out, sem.at[0])]
    copies.append(pltpu.make_async_copy(mobility_in, mobility_out, sem.at[1]))
    for i in range(grad_in.shape[0]):
        copies.append(pltpu.make_async_copy(grad_in.at[i], grad_out.at[i], sem.at[2 + i]))
    for copy in copies:
        copy.start()
    for copy in copies:
        copy.wait()


def body(slabs, phase_noise, labels, solute, mobility, cotangent, adj_solute):
    _, orders, layers, rows, lanes = phase_noise.shape
    sub = labels.shape[0]
    span = layers // PAIRS
    tile = (rows, lanes)

    def vmem(*lead):
        return pltpu.VMEM(lead + tile, jnp.float32)

    in_hbm = pl.BlockSpec(memory_space=pltpu.HBM)
    in_vmem = pl.BlockSpec(memory_space=pltpu.VMEM)
    elements = orders * layers * rows * lanes
    grad, solute_gradient, mobility_gradient = pl.pallas_call(
        functools.partial(kernel, slabs),
        out_shape=(
            jax.ShapeDtypeStruct(phase_noise.shape[1:], jnp.float32),
            jax.ShapeDtypeStruct(solute.shape, jnp.float32),
            jax.ShapeDtypeStruct((1, mobility.shape[0]), jnp.float32),
        ),
        in_specs=[in_hbm] * 6,
        out_specs=(in_vmem,) * 3,
        scratch_shapes=[
            pltpu.SMEM(mobility.shape, jnp.float32),
            vmem(orders, layers + 2), vmem(orders, layers + 2), vmem(orders, layers + 2),
            vmem(orders, layers), vmem(orders, layers), vmem(orders, layers), vmem(orders),
            pltpu.VMEM((layers,) + tile, jnp.int32), pltpu.VMEM((2,) + tile, jnp.int32),
            vmem(span), vmem(span + 2), vmem(span + 2), vmem(span + 2),
            vmem(PAIRS, span), vmem(GROUPS, span), vmem(2, span), vmem(PAIRS, span),
            vmem(PAIRS, span, 5), vmem(GROUPS, span, 5), vmem(2, 2, span), vmem(PAIRS, 2, span),
            vmem(PAIRS, span), vmem(GROUPS, span), vmem(2, span), vmem(PAIRS, span),
            pltpu.VMEM((orders, lanes), jnp.float32),
            pltpu.VMEM((max(slabs - 1, 1), orders, lanes), jnp.float32),
            pltpu.VMEM((GROUPS, orders, lanes), jnp.float32),
            vmem(span),
            pltpu.SemaphoreType.DMA((6,)),
            pltpu.SemaphoreType.DMA((9, GROUPS)),
            pltpu.SemaphoreType.DMA((9, GROUPS)),
            pltpu.SemaphoreType.DMA((9, 2)),
            pltpu.SemaphoreType.DMA((9, 2)),
            pltpu.SemaphoreType.DMA((max(slabs - 1, 1),)),
            pltpu.SemaphoreType.DMA((max(slabs - 1, 1),)),
        ],
        compiler_params=pltpu.CompilerParams(
            collective_id=0, has_side_effects=True, vmem_limit_bytes=VMEM_LIMIT
        ),
        cost_estimate=pl.CostEstimate(flops=100 * elements, bytes_accessed=12 * elements, transcendentals=0),
    )(*(pltpu.with_memory_space_constraint(x, pltpu.HBM) for x in (phase_noise[0], labels, solute, mobility, cotangent[0], adj_solute)))
    grad, solute_gradient, mobility_gradient = pl.pallas_call(
        hand_over,
        out_shape=tuple(jax.ShapeDtypeStruct(x.shape, x.dtype) for x in (grad, solute_gradient, mobility_gradient)),
        in_specs=[in_vmem] * 3,
        out_specs=(in_hbm,) * 3,
        scratch_shapes=[pltpu.SemaphoreType.DMA((orders + 2,))],
        compiler_params=pltpu.CompilerParams(vmem_limit_bytes=VMEM_LIMIT),
        cost_estimate=pl.CostEstimate(flops=0, bytes_accessed=8 * elements, transcendentals=0),
    )(grad, solute_gradient, mobility_gradient)
    return grad[None], solute_gradient, mobility_gradient.reshape(-1)


def solution(mesh):
    slabs = mesh.shape["space"] // GROUPS
    fields = P(("runs", "space"), None, None, None, None)
    cells = P(("runs", "space"), None, None)
    return jax.shard_map(
        functools.partial(body, slabs),
        mesh=mesh,
        in_specs=(fields, cells, cells, P(), fields, cells),
        out_specs=(fields, cells, P("runs")),
        check_vma=False,
    )
```

```python
import functools

import jax
import jax.numpy as jnp
from jax import lax
from jax.experimental import pallas as pl
from jax.experimental.pallas import tpu as pltpu
from jax.sharding import PartitionSpec as P

P_SIZE = 64
GROUPS = 8

time_step = 0.1
gradient_coef = 0.75
coupling = 1.5
chem_height = 2.5
alpha_level = 0.2
beta_level = 0.8
solute_mobility = 0.3
epsilon = 1e-05

MESH = pl.DeviceIdType.MESH
CUBIC = 1.0 - 2.0 * coupling
GAP = beta_level - alpha_level
BETA_GROUP = GROUPS // 2
PAIRS = GROUPS // 2
VMEM_LIMIT = 16 * 1024 * 1024

LABELS, SUM_A, COEF_A, SUM_B, COEF_B, SUM_C, COEF_C, MOBILITY, SUM_END = range(9)
PHASE_RIM, ADJ_RIM, BAR_RIM, ADJ_RING, POT_RING, BAR_RING, GIVE, GIVE_BACK, LABEL_RIM = range(9)


def turn(x):
    last = x.ndim - 1
    lanes, rows = x.shape[-1], x.shape[-2]
    across = pltpu.roll(x, 1, last) + pltpu.roll(x, lanes - 1, last)
    return across + (pltpu.roll(x, 1, last - 1) + pltpu.roll(x, rows - 1, last - 1))


def curve(ref, layer):
    middle = ref[:, layer + 1]
    return (ref[:, layer] + ref[:, layer + 2] - 6.0 * middle) + turn(middle)


def curve_cells(ref):
    middle = ref[1:-1]
    return (ref[:-2] + ref[2:] - 6.0 * middle) + turn(middle)


def kernel(
    slabs, noise_ref, labels_ref, solute_ref, mobility_hbm, adj_ref, adjc_ref,
    grad_ref, solgrad_ref, mobgrad_ref,
    mobility_ref, phi, lam, bar, phi1, drive, pre, rate_buf, lab, lab_rim, conc, adjc, pot, adjc1,
    sum_a, got_a, put_a, coef_a, sum_b, got_b, put_b, coef_b, sum_c, got_c, put_c, coef_c,
    mob_mine, mob_slabs, mob_all, solgrad,
    load_sem, send_sem, recv_sem, rim_send, rim_recv, mob_send, mob_recv,
):
    orders, layers = noise_ref.shape[0], noise_ref.shape[1]
    sub = layers // GROUPS
    span = layers // PAIRS
    place = lax.axis_index("space")
    count = slabs * GROUPS
    group = lax.rem(place, GROUPS)
    slab = lax.div(place, GROUPS)
    base = slab * GROUPS
    pair = lax.div(group, 2)
    second = lax.rem(group, 2)
    owner = second == 1
    above, below = lax.rem(place + GROUPS, count), lax.rem(place + count - GROUPS, count)

    def pair_at(j):
        high = lax.rem(lax.div(pair, 2) + lax.div(j, 2), 2)
        low = lax.rem(lax.rem(pair, 2) + lax.rem(j, 2), 2)
        return 2 * high + low

    def far_pairs():
        return [pair_at(jnp.int32(j)) for j in range(PAIRS - 1, 0, -1)]

    def others():
        return [2 * q + c for q in far_pairs() for c in range(2)] + [2 * pair + 1 - second]

    def other_slab(s):
        return lax.rem(slab + s, slabs) * GROUPS + group

    def shifted(by):
        return lax.rem(place + count + by, count)

    barrier = pltpu.get_barrier_semaphore()

    def greet(device):
        pl.semaphore_signal(barrier, inc=1, device_id={"space": device}, device_id_type=MESH)

    for s in range(1, slabs):
        greet(other_slab(s))

    @pl.when(owner)
    def _():
        for by in (2, -2, 1):
            greet(shifted(by))

    for g in others():
        greet(base + g)

    load_labels = pltpu.make_async_copy(labels_ref, lab.at[pl.ds(group * sub, sub)], load_sem.at[0])
    load_noise = pltpu.make_async_copy(noise_ref, phi.at[:, pl.ds(1, layers)], load_sem.at[1])
    load_adjc = pltpu.make_async_copy(adjc_ref, adjc.at[pl.ds(1 + second * sub, sub)], load_sem.at[2])
    load_solute = pltpu.make_async_copy(solute_ref, conc.at[pl.ds(second * sub, sub)], load_sem.at[3])
    load_adj = pltpu.make_async_copy(adj_ref, lam.at[:, pl.ds(1, layers)], load_sem.at[4])
    load_mobility = pltpu.make_async_copy(mobility_hbm, mobility_ref, load_sem.at[5])
    for load in (load_mobility, load_labels, load_noise, load_adjc, load_solute, load_adj):
        load.start()
    load_mobility.wait()
    for i in range(orders):
        rate_buf[i] = jnp.full(rate_buf.shape[1:], time_step * mobility_ref[group * orders + i], jnp.float32)

    pl.semaphore_wait(barrier, GROUPS - 1 + slabs - 1 + 1 + second)

    def to_group(kind, src, dst, g, slot):
        return pltpu.make_async_remote_copy(
            src_ref=src, dst_ref=dst, send_sem=send_sem.at[kind, g], recv_sem=recv_sem.at[kind, slot],
            device_id={"space": base + g}, device_id_type=MESH,
        )

    def arrived(kind, dst, slot):
        to_group(kind, dst, dst, 2 * pair + 1 - second, slot).wait_recv()

    def sent(kind, src, g):
        to_group(kind, src, src, g, g).wait_send()

    def rim_copy(kind, side, src, dst, device):
        return pltpu.make_async_remote_copy(
            src_ref=src, dst_ref=dst, send_sem=rim_send.at[kind, side], recv_sem=rim_recv.at[kind, side],
            device_id={"space": device}, device_id_type=MESH,
        )

    def rims_of(kind, src, ref, offset):
        last = layers + 1
        return (
            rim_copy(kind, 0, src.at[:, layers - 1 + offset], ref.at[:, 0], above),
            rim_copy(kind, 1, src.at[:, offset], ref.at[:, last], below),
        )

    def ring_of(kind, ref):
        return (
            rim_copy(kind, 0, ref.at[span], ref.at[0], shifted(2)),
            rim_copy(kind, 1, ref.at[1], ref.at[span + 1], shifted(-2)),
        )

    sibling = shifted(1 - 2 * second)
    adj_down = rim_copy(ADJ_RING, 1, adjc_ref.at[0], adjc.at[span + 1], shifted(-1))
    adj_up = rim_copy(ADJ_RING, 0, adjc_ref.at[sub - 1], adjc.at[0], shifted(2))
    give_adjc = rim_copy(GIVE, 0, adjc_ref, adjc.at[pl.ds(1, sub)], sibling)
    give_solute = rim_copy(GIVE, 1, solute_ref, conc.at[pl.ds(0, sub)], sibling)
    pot_ring = ring_of(POT_RING, pot)
    bar_ring = ring_of(BAR_RING, adjc1)
    give_solgrad = rim_copy(GIVE_BACK, 0, solgrad.at[pl.ds(0, sub)], solgrad.at[pl.ds(0, sub)], sibling)

    for g in others():
        to_group(LABELS, labels_ref, lab.at[pl.ds(group * sub, sub)], g, group).start()

    @pl.when(owner)
    def _():
        adj_up.start()

    @pl.when(second == 0)
    def _():
        give_solute.start()
        give_adjc.start()
        adj_down.start()

    phase_rim = rims_of(PHASE_RIM, noise_ref, phi, 0)
    adj_rim = rims_of(ADJ_RIM, adj_ref, lam, 0)
    label_rim = (
        rim_copy(LABEL_RIM, 0, lab.at[layers - 1], lab_rim.at[0], above),
        rim_copy(LABEL_RIM, 1, lab.at[0], lab_rim.at[1], below),
    )
    for copy in phase_rim:
        copy.start()

    def labels_from(g):
        arrived(LABELS, lab.at[pl.ds(g * sub, sub)], g)

    def over_layers(q, act):
        for k in range(span):
            act(q * span + k, k)

    def give_sum(kind, sums, got, q):
        to_group(kind, sums.at[q], got.at[group], 2 * q + 1, group).start()

    def over_pairs(kind, sums, got, chunk, carry):
        def run(i, carry):
            q = pair_at(PAIRS - 1 - i)
            carry = chunk(q, True, carry)
            give_sum(kind, sums, got, q)
            return carry

        carry = lax.fori_loop(0, PAIRS - 1, run, carry)
        carry = chunk(pair, False, carry)

        @pl.when(second == 0)
        def _():
            give_sum(kind, sums, got, pair)

        @pl.when(owner)
        def _():
            got[group] = sums[pair]

        return carry

    def all_sums(kind, got):
        for g in others():
            arrived(kind, got.at[g], g)

    def give_coef(kind, put, coef):
        for g in others():
            to_group(kind, put.at[lax.div(g, BETA_GROUP)], coef.at[pair], g, pair).start()
        coef[pair] = put[lax.div(group, BETA_GROUP)]

    def own_coef(kind, coef):
        @pl.when(second == 0)
        def _():
            arrived(kind, coef.at[pair], pair)

    def started(at, label):
        ids = group * orders + lax.broadcasted_iota(jnp.int32, rate_buf.shape, 0)
        field = phi[:, at] + jnp.where(label[None] == ids, 0.5, 0.0)
        phi[:, at] = field
        return field

    def start_chunk(q, far, carry):
        if far:
            labels_from(2 * q)
            labels_from(2 * q + 1)
        else:
            labels_from(2 * pair + 1 - second)

        @pl.when(q == PAIRS - 1)
        def _():
            label_rim[0].start()

        @pl.when(q == 0)
        def _():
            label_rim[1].start()

        def layer(z, k):
            field = started(z + 1, lab[z])
            sum_a[q, k] = jnp.sum(field * field, axis=0)

        over_layers(q, layer)
        return carry

    load_labels.wait()
    load_noise.wait()
    over_pairs(SUM_A, sum_a, got_a, start_chunk, 0)

    def local_layer(z):
        field, rate = phi[:, z + 1], rate_buf[...]
        push = CUBIC * field * field * field - gradient_coef * curve(phi, z)
        drive[:, z] = push
        known = field - rate * push
        phi1[:, z] = known
        scaled, adj = rate * field, rate * lam[:, z + 1]
        q, k = z // span, z % span
        sum_b[q, k, 0] = jnp.sum(known * known, axis=0)
        sum_b[q, k, 1] = jnp.sum(scaled * known, axis=0)
        sum_b[q, k, 2] = jnp.sum(scaled * scaled, axis=0)
        sum_b[q, k, 3] = jnp.sum(adj * known, axis=0)
        sum_b[q, k, 4] = jnp.sum(adj * scaled, axis=0)

    def inner_part(q):
        first = 1 if q == 0 else 0
        return pl.ds(first, span - 1 if q in (0, PAIRS - 1) else span)

    def end_part(q):
        return pl.ds(0 if q == 0 else span - 1, 1)

    def give_part(kind, q, part):
        @pl.when(2 * q + 1 != group)
        def _():
            to_group(kind, sum_b.at[q, part], got_b.at[group, part], 2 * q + 1, group).start()

        @pl.when(2 * q + 1 == group)
        def _():
            got_b[group, part] = sum_b[q, part]

    def sent_part(kind, q, part):
        @pl.when(2 * q + 1 != group)
        def _():
            sent(kind, sum_b.at[q, part], 2 * q + 1)

    def over_inner(act):
        def run(z, carry):
            act(z)
            return carry

        lax.fori_loop(1, layers - 1, run, 0)

    load_adj.wait()

    for q in (0, PAIRS - 1) + tuple(range(1, PAIRS - 1)):
        first = max(q * span, 1)
        last = min((q + 1) * span, layers - 1)

        def run(z, carry):
            local_layer(z)
            return carry

        lax.fori_loop(first, last, run, 0)
        give_part(SUM_B, q, inner_part(q))

    load_adjc.wait()
    load_solute.wait()

    def total_of(parts):
        low, high = parts[0], parts[BETA_GROUP]
        for g in range(1, BETA_GROUP):
            low = low + parts[g]
            high = high + parts[BETA_GROUP + g]
        return low + high, high

    def state_of(squares, beta_squares, c):
        inverse = 1.0 / (squares + epsilon)
        share = beta_squares * inverse
        slope = chem_height * ((c - beta_level) ** 2 - (c - alpha_level) ** 2)
        pull = 2.0 * slope * inverse
        plain = 2.0 * coupling * squares - 1.0 - pull * share
        return inverse, share, pull, plain

    def adjoint_of(state, moment, beta_moment, pot_bar):
        inverse, share, pull, _ = state
        scaled = pull * inverse
        pot_part = (2.0 * chem_height * GAP) * inverse * pot_bar
        all_bar = 2.0 * coupling * moment - scaled * (beta_moment - 2.0 * share * moment) + share * pot_part
        beta_bar = -scaled * moment - pot_part
        c_bar = (-4.0 * chem_height * GAP) * inverse * (beta_moment - share * moment) + 2.0 * chem_height * pot_bar
        return 2.0 * all_bar, 2.0 * (all_bar + beta_bar), c_bar

    @pl.when(owner)
    def _():
        give_solute.wait_recv()
        all_sums(SUM_A, got_a)
        state = state_of(*total_of(got_a), conc[...])
        put_a[0] = state[3]
        put_a[1] = state[3] + state[2]
        pot[1 : span + 1] = 2.0 * chem_height * (conc[...] - alpha_level - state[1] * GAP)
        for copy in pot_ring:
            copy.start()

    for copy in phase_rim + label_rim:
        copy.wait_recv()
    started(0, lab_rim[0])
    started(layers + 1, lab_rim[1])

    for q in (0, PAIRS - 1):
        local_layer(q * (layers - 1) // (PAIRS - 1))
        give_part(SUM_END, q, end_part(q))

    for copy in adj_rim:
        copy.start()

    @pl.when(owner)
    def _():
        give_coef(COEF_A, put_a, coef_a)

    @pl.when(owner)
    def _():
        for copy in (give_adjc, adj_up, adj_down) + pot_ring:
            copy.wait_recv()
        pot_bar = (time_step * solute_mobility) * curve_cells(adjc)
        conc1 = conc[...] + (time_step * solute_mobility) * curve_cells(pot)
        for q in range(PAIRS):

            @pl.when(pair == q)
            def _():
                for g in others():
                    arrived(SUM_B, got_b.at[g, inner_part(q)], g)
                if q in (0, PAIRS - 1):
                    for g in others():
                        arrived(SUM_END, got_b.at[g, end_part(q)], g)

        def plane(first, a):
            parts = [got_b[first] + got_b[first + 1], got_b[first + 2] + got_b[first + 3]]
            sums = parts[0] + parts[1]
            return sums[:, 0] - a * (2.0 * sums[:, 1] - a * sums[:, 2]), a * sums[:, 4] - sums[:, 3]

        low_squares, low_moment = plane(0, put_a[0])
        squares, moment = plane(BETA_GROUP, put_a[1])
        state = state_of(low_squares + squares, squares, conc1)
        plain, beta, c_bar = adjoint_of(state, low_moment + moment, moment, pot_bar)
        put_b[0, 0] = state[3]
        put_b[0, 1] = plain
        put_b[1, 0] = state[3] + state[2]
        put_b[1, 1] = beta
        give_coef(COEF_B, put_b, coef_b)
        adjc1[1 : span + 1] = adjc[1 : span + 1] + c_bar
        for copy in bar_ring:
            copy.start()

    def step_chunk(q):
        def layer(z, k):
            part = phi[:, z + 1] * coef_a[q, k][None]
            drive[:, z] = drive[:, z] + part
            phi1[:, z] = phi1[:, z] - rate_buf[...] * part

        over_layers(q, layer)

    own_coef(COEF_A, coef_a)
    step_chunk(pair)

    def step_pair(j, carry):
        q = pair_at(j)
        arrived(COEF_A, coef_a.at[q], q)
        step_chunk(q)
        return carry

    lax.fori_loop(1, PAIRS, step_pair, 0)

    def local_bar(z, moved):
        adj, field, rate = lam[:, z + 1], phi1[:, z], rate_buf[...]
        curved = gradient_coef * curve(lam, z)
        squared = field * field
        pre[:, z] = adj + rate * (curved - (3.0 * CUBIC) * squared * adj)
        return moved + field * (CUBIC * squared * adj - curved)

    moved = lax.fori_loop(1, layers - 1, local_bar, jnp.zeros(rate_buf.shape, jnp.float32))

    for copy in adj_rim:
        copy.wait_recv()
    moved = local_bar(0, moved)
    moved = local_bar(layers - 1, moved)

    def bar_chunk(q, moved):
        for k in range(span):
            z = q * span + k
            adj, field, rate = lam[:, z + 1], phi1[:, z], rate_buf[...]
            scaled = adj * coef_b[q, 0, k][None]
            full = pre[:, z] + field * coef_b[q, 1, k][None] - rate * scaled
            bar[:, z + 1] = full
            sum_c[q, k] = -jnp.sum(rate * full * phi[:, z + 1], axis=0)
            moved = moved + (field * scaled + full * drive[:, z])
        return moved

    bar_rim = rims_of(BAR_RIM, bar, bar, 1)

    def end_pair_sums(q):
        @pl.when(2 * q + 1 != group)
        def _():
            give_sum(SUM_C, sum_c, got_c, q)

        @pl.when(2 * q + 1 == group)
        def _():
            got_c[group] = sum_c[q]

    for step, q in enumerate((PAIRS - 1, 0) + tuple(range(1, PAIRS - 1))):

        @pl.when(2 * q + 1 != group)
        def _():
            arrived(COEF_B, coef_b.at[q], q)

        moved = bar_chunk(q, moved)
        end_pair_sums(q)
        if step < 2:
            bar_rim[step].start()
    mob_mine[...] = -time_step * jnp.sum(moved, axis=1)
    mob_copies = [
        pltpu.make_async_remote_copy(
            src_ref=mob_mine, dst_ref=mob_slabs.at[s - 1], send_sem=mob_send.at[s - 1], recv_sem=mob_recv.at[s - 1],
            device_id={"space": other_slab(s)}, device_id_type=MESH,
        )
        for s in range(1, slabs)
    ]
    for copy in mob_copies:
        copy.start()

    def local_grad(z):
        full, field, rate = bar[:, z + 1], phi[:, z + 1], rate_buf[...]
        slope = coef_a[z // span, z % span][None] + (3.0 * CUBIC) * field * field
        pre[:, z] = full + rate * (gradient_coef * curve(bar, z) - full * slope)

    over_inner(local_grad)

    @pl.when(owner)
    def _():
        for copy in bar_ring:
            copy.wait_recv()
        pot_bar = (time_step * solute_mobility) * curve_cells(adjc1)
        state = state_of(*total_of(got_a), conc[...])
        all_sums(SUM_C, got_c)
        plain, beta, c_bar = adjoint_of(state, *total_of(got_c), pot_bar)
        put_c[0] = plain
        put_c[1] = beta
        give_coef(COEF_C, put_c, coef_c)
        solgrad[...] = adjc1[1 : span + 1] + c_bar
        give_solgrad.start()

    for copy in mob_copies:
        copy.wait_recv()
    whole = mob_mine[...]
    for s in range(1, slabs):
        whole = whole + mob_slabs[s - 1]
    mob_all[group] = whole
    for g in others():
        to_group(MOBILITY, mob_all.at[group], mob_all.at[group], g, group).start()

    for copy in bar_rim:
        copy.wait_recv()
    local_grad(0)
    local_grad(layers - 1)

    def grad_chunk(q):
        def layer(z, k):
            grad_ref[:, z] = pre[:, z] + phi[:, z + 1] * coef_c[q, k][None]

        over_layers(q, layer)

    own_coef(COEF_C, coef_c)
    grad_chunk(pair)

    def grad_pair(j, carry):
        q = pair_at(j)
        arrived(COEF_C, coef_c.at[q], q)
        grad_chunk(q)
        return carry

    lax.fori_loop(1, PAIRS, grad_pair, 0)

    @pl.when(second == 0)
    def _():
        give_solgrad.wait_recv()

    solgrad_ref[...] = solgrad[pl.ds(second * sub, sub)]
    for g in others():
        arrived(MOBILITY, mob_all.at[g], g)
    table = mob_all[...].reshape(GROUPS * orders, mob_all.shape[-1])
    mobgrad_ref[...] = jnp.sum(table.T, axis=0, keepdims=True)

    for q in range(PAIRS):
        sent_part(SUM_B, q, inner_part(q))
        if q in (0, PAIRS - 1):
            sent_part(SUM_END, q, end_part(q))
    for g in others():
        sent(LABELS, labels_ref, g)
        sent(MOBILITY, mob_all.at[group], g)
    for q in far_pairs():
        sent(SUM_A, sum_a.at[q], 2 * q + 1)
        sent(SUM_C, sum_c.at[q], 2 * q + 1)

    @pl.when(second == 0)
    def _():
        for copy in (give_solute, give_adjc, adj_down):
            copy.wait_send()
        sent(SUM_A, sum_a.at[pair], 2 * pair + 1)
        sent(SUM_C, sum_c.at[pair], 2 * pair + 1)

    @pl.when(owner)
    def _():
        for copy in (adj_up, give_solgrad) + pot_ring + bar_ring:
            copy.wait_send()
        for g in others():
            sent(COEF_A, put_a.at[0], g)
            sent(COEF_B, put_b.at[0], g)
            sent(COEF_C, put_c.at[0], g)

    for copy in adj_rim + phase_rim + label_rim + bar_rim + tuple(mob_copies):
        copy.wait_send()


def hand_over(grad_in, solute_in, mobility_in, grad_out, solute_out, mobility_out, sem):
    copies = [pltpu.make_async_copy(solute_in, solute_out, sem.at[0])]
    copies.append(pltpu.make_async_copy(mobility_in, mobility_out, sem.at[1]))
    for i in range(grad_in.shape[0]):
        copies.append(pltpu.make_async_copy(grad_in.at[i], grad_out.at[i], sem.at[2 + i]))
    for copy in copies:
        copy.start()
    for copy in copies:
        copy.wait()


def body(slabs, phase_noise, labels, solute, mobility, cotangent, adj_solute):
    _, orders, layers, rows, lanes = phase_noise.shape
    sub = labels.shape[0]
    span = layers // PAIRS
    tile = (rows, lanes)

    def vmem(*lead):
        return pltpu.VMEM(lead + tile, jnp.float32)

    in_hbm = pl.BlockSpec(memory_space=pltpu.HBM)
    in_vmem = pl.BlockSpec(memory_space=pltpu.VMEM)
    elements = orders * layers * rows * lanes
    grad, solute_gradient, mobility_gradient = pl.pallas_call(
        functools.partial(kernel, slabs),
        out_shape=(
            jax.ShapeDtypeStruct(phase_noise.shape[1:], jnp.float32),
            jax.ShapeDtypeStruct(solute.shape, jnp.float32),
            jax.ShapeDtypeStruct((1, mobility.shape[0]), jnp.float32),
        ),
        in_specs=[in_hbm] * 6,
        out_specs=(in_vmem,) * 3,
        scratch_shapes=[
            pltpu.SMEM(mobility.shape, jnp.float32),
            vmem(orders, layers + 2), vmem(orders, layers + 2), vmem(orders, layers + 2),
            vmem(orders, layers), vmem(orders, layers), vmem(orders, layers), vmem(orders),
            pltpu.VMEM((layers,) + tile, jnp.int32), pltpu.VMEM((2,) + tile, jnp.int32),
            vmem(span), vmem(span + 2), vmem(span + 2), vmem(span + 2),
            vmem(PAIRS, span), vmem(GROUPS, span), vmem(2, span), vmem(PAIRS, span),
            vmem(PAIRS, span, 5), vmem(GROUPS, span, 5), vmem(2, 2, span), vmem(PAIRS, 2, span),
            vmem(PAIRS, span), vmem(GROUPS, span), vmem(2, span), vmem(PAIRS, span),
            pltpu.VMEM((orders, lanes), jnp.float32),
            pltpu.VMEM((max(slabs - 1, 1), orders, lanes), jnp.float32),
            pltpu.VMEM((GROUPS, orders, lanes), jnp.float32),
            vmem(span),
            pltpu.SemaphoreType.DMA((6,)),
            pltpu.SemaphoreType.DMA((9, GROUPS)),
            pltpu.SemaphoreType.DMA((9, GROUPS)),
            pltpu.SemaphoreType.DMA((9, 2)),
            pltpu.SemaphoreType.DMA((9, 2)),
            pltpu.SemaphoreType.DMA((max(slabs - 1, 1),)),
            pltpu.SemaphoreType.DMA((max(slabs - 1, 1),)),
        ],
        compiler_params=pltpu.CompilerParams(
            collective_id=0, has_side_effects=True, vmem_limit_bytes=VMEM_LIMIT
        ),
        cost_estimate=pl.CostEstimate(flops=100 * elements, bytes_accessed=12 * elements, transcendentals=0),
    )(*(pltpu.with_memory_space_constraint(x, pltpu.HBM) for x in (phase_noise[0], labels, solute, mobility, cotangent[0], adj_solute)))
    grad, solute_gradient, mobility_gradient = pl.pallas_call(
        hand_over,
        out_shape=tuple(jax.ShapeDtypeStruct(x.shape, x.dtype) for x in (grad, solute_gradient, mobility_gradient)),
        in_specs=[in_vmem] * 3,
        out_specs=(in_hbm,) * 3,
        scratch_shapes=[pltpu.SemaphoreType.DMA((orders + 2,))],
        compiler_params=pltpu.CompilerParams(vmem_limit_bytes=VMEM_LIMIT),
        cost_estimate=pl.CostEstimate(flops=0, bytes_accessed=8 * elements, transcendentals=0),
    )(grad, solute_gradient, mobility_gradient)
    return grad[None], solute_gradient, mobility_gradient.reshape(-1)


def solution(mesh):
    slabs = mesh.shape["space"] // GROUPS
    fields = P(("runs", "space"), None, None, None, None)
    cells = P(("runs", "space"), None, None)
    return jax.shard_map(
        functools.partial(body, slabs),
        mesh=mesh,
        in_specs=(fields, cells, cells, P(), fields, cells),
        out_specs=(fields, cells, P("runs")),
        check_vma=False,
    )
```
